128 devices in a mesh: dp: 16 (over y, z_hi, core), tensor: 8 (over z_lo, x).
Axes of the slice: x: 4, y: 4, z: 4 (z_hi: 2, z_lo: 2; z = z_hi * 2 + z_lo), core: 2. Of those that a mesh axis runs over, the one named last changes fastest.
Arguments:
- teacher_hidden: bfloat16 [2048, 16384], P(None, 'dp'), may hold values from -400 to 400
- attn_gain: float32 [1, 16384], P(None, 'dp'), may hold values from 0.5 to 6
- w_query: bfloat16 [1, 16384, 8192], P(None, 'dp', 'tensor'), may hold values from -0.046875 to 0.046875
- key_projection: bfloat16 [1, 16384, 1024], P(None, 'dp', 'tensor'), may hold values from -0.046875 to 0.046875
- value_projection: bfloat16 [1, 16384, 1024], P(None, 'dp', 'tensor'), may hold values from -0.046875 to 0.046875
- w_out: bfloat16 [1, 8192, 16384], P(None, 'tensor', 'dp'), may hold values from -0.0625 to 0.0625
- student_hidden: bfloat16 [2048, 4096], P(None, 'tensor'), may hold values from -6 to 6
- w_proj: bfloat16 [4096, 16384], P('tensor', 'dp'), may hold values from -0.09375 to 0.09375
Outputs:
- teacher_out: bfloat16 [2048, 16384], P(None, 'dp')
- distill_loss: float32 [], replicated
- proj_grad: float32 [4096, 16384], P('tensor', 'dp')
- student_grad: float32 [2048, 4096], P('dp', 'tensor')
The draws below stay inside these ranges and needn't reach their ends.
All inputs are finite; a program needn't handle non-finite values.
Results may differ from the reference program's by a relative error of at most 0.035.
Values may be sent and summed in bfloat16 or wider, within the bound.
No kernel may reach another device: no remote copies, remote signals or barrier semaphores. Data moves between devices by JAX's collectives and lax.ppermute only.
A program may use at most 128 MiB of HBM per device.

```python
import math
import jax
import jax.numpy as jnp
from jax import lax

MODEL_WIDTH = 16384
DS = 4096
QUERY_HEADS = 64
KEY_VALUE_HEADS = 8
HEAD_SIZE = 128
TEACHER_LAYERS = 1
TOKENS = 2048
SEQ_LEN = 2048
N_TENSOR = 8


def draw_teacher_hidden(key, part):
    key = jax.random.fold_in(key, 11)
    key_entries, key_rows, key_columns = jax.random.split(key, 3)
    entries = jnp.clip(jax.random.normal(key_entries, (TOKENS, MODEL_WIDTH), jnp.float32), -4.0, 4.0)
    row_scale = 10.0 ** jax.random.uniform(key_rows, (TOKENS, 1), jnp.float32)
    col_scale = 10.0 ** jax.random.uniform(key_columns, (1, MODEL_WIDTH), jnp.float32)
    rising = 3.0 ** (jnp.arange(MODEL_WIDTH, dtype=jnp.float32)[None, :] / MODEL_WIDTH)
    return (0.3 * entries * row_scale * col_scale * rising).astype(jnp.bfloat16)


def draw_attn_gain(key, part):
    key = jax.random.fold_in(key, 23)
    return jnp.exp(jax.random.uniform(key, (TEACHER_LAYERS, MODEL_WIDTH), jnp.float32, math.log(0.5), math.log(2.0)))


def shard_levels(rng, dims, cuts, smallest, largest):
    level = 1.0
    for dim, shards_of in cuts:
        heights = jax.random.uniform(jax.random.fold_in(jax.random.fold_in(rng, 6), dim), (shards_of,), jnp.float32, smallest / len(cuts), largest / len(cuts))
        level = level * jnp.repeat(jnp.exp(heights), dims[dim] // shards_of).reshape((-1,) + (1,) * (len(dims) - 1 - dim))
    return level


def centred(own_key, dims, scale, bound, pieces=(), held_as=jnp.bfloat16):
    values = jax.random.normal(own_key, dims, jnp.float32) * scale
    if len(pieces) > 0:
        values = shard_levels(own_key, dims, pieces, -0.22, 0.18) * values
    return jnp.clip(values, min=-bound, max=bound).astype(held_as)


def setup_inputs(seed: int = 0) -> dict:
    key_list = jax.random.split(jax.random.key(seed), 9)
    return {
        "teacher_hidden": draw_teacher_hidden(jax.random.fold_in(key_list[8], 71), 0),
        "attn_gain": draw_attn_gain(jax.random.fold_in(key_list[8], 71), 0),
        "w_query": centred(key_list[2], (TEACHER_LAYERS, MODEL_WIDTH, QUERY_HEADS * HEAD_SIZE), MODEL_WIDTH ** -0.5, 0.046875, ((1, 16), (2, 8))),
        "key_projection": centred(key_list[3], (TEACHER_LAYERS, MODEL_WIDTH, KEY_VALUE_HEADS * HEAD_SIZE), MODEL_WIDTH ** -0.5, 0.046875, ((1, 16), (2, 8))),
        "value_projection": centred(key_list[4], (TEACHER_LAYERS, MODEL_WIDTH, KEY_VALUE_HEADS * HEAD_SIZE), MODEL_WIDTH ** -0.5, 0.046875, ((1, 16), (2, 8))),
        "w_out": centred(key_list[5], (TEACHER_LAYERS, QUERY_HEADS * HEAD_SIZE, MODEL_WIDTH), (QUERY_HEADS * HEAD_SIZE) ** -0.5, 0.0625, ((1, 8), (2, 16))),
        "student_hidden": centred(key_list[6], (TOKENS, DS), 1.0, 6.0, ((1, 8),)),
        "w_proj": centred(key_list[7], (DS, MODEL_WIDTH), DS ** -0.5, 0.09375, ((0, 8), (1, 16))),
    }


epsilon = 1e-05

def rms_normed(hidden, gain_row):
    widened = hidden.astype(jnp.float32)
    inv_scale = lax.rsqrt(lax.optimization_barrier(jnp.sum(widened * widened, axis=1)) / MODEL_WIDTH + epsilon)
    return (widened * inv_scale[:, None] * gain_row[None, :]).astype(jnp.bfloat16)

def attend(packed, query_cols, key_columns):
    row_count = packed.shape[0]
    seq_count = row_count // SEQ_LEN
    query_groups = QUERY_HEADS // KEY_VALUE_HEADS
    kv_heads = key_columns // HEAD_SIZE
    queries = packed[:, :query_cols].reshape(seq_count, SEQ_LEN, kv_heads, query_groups, HEAD_SIZE)
    key_rows = packed[:, query_cols:query_cols + key_columns].reshape(seq_count, SEQ_LEN, kv_heads, HEAD_SIZE)
    value_rows = packed[:, query_cols + key_columns:].reshape(seq_count, SEQ_LEN, kv_heads, HEAD_SIZE)
    queries = jnp.transpose(queries, (2, 0, 1, 3, 4))
    key_rows = jnp.transpose(key_rows, (2, 0, 1, 3))
    value_rows = jnp.transpose(value_rows, (2, 0, 1, 3))
    future_mask = lax.broadcasted_iota(jnp.int32, (SEQ_LEN, SEQ_LEN), 1) > lax.broadcasted_iota(jnp.int32, (SEQ_LEN, SEQ_LEN), 0)

    def one_head(operands):
        head_queries, head_keys, head_values = operands
        scores = jnp.einsum('ntgd,nsd->ngts', head_queries.astype(jnp.float32), head_keys.astype(jnp.float32)) / math.sqrt(HEAD_SIZE)
        scores = jnp.where(future_mask, -jnp.inf, scores)
        row_max = lax.optimization_barrier(jnp.max(scores, axis=-1, keepdims=True))
        exp_scores = jnp.exp(scores - row_max)
        weights = (exp_scores / lax.optimization_barrier(jnp.sum(exp_scores, axis=-1, keepdims=True))).astype(jnp.bfloat16)
        blended = jnp.einsum('ngts,nsd->ntgd', weights.astype(jnp.float32), head_values.astype(jnp.float32))
        return blended.astype(jnp.bfloat16)
    blended = lax.map(one_head, (queries, key_rows, value_rows))
    blended = jnp.transpose(blended, (1, 2, 0, 3, 4))
    return blended.reshape(row_count, query_cols)

def blocked_sum(left, right, blocks):
    block_width = left.shape[1] // blocks
    total = jnp.zeros((left.shape[0], right.shape[1]), jnp.float32)
    for block_index in range(blocks):
        term = jnp.dot(left[:, block_index * block_width:(block_index + 1) * block_width], right[block_index * block_width:(block_index + 1) * block_width], preferred_element_type=jnp.float32)
        rounded = lax.optimization_barrier(term.astype(jnp.bfloat16))
        total = total + rounded.astype(jnp.float32)
    return total

def reference(teacher_hidden, attn_gain, w_query, key_projection, value_projection, w_out, student_hidden, w_proj):
    hidden = teacher_hidden
    query_cols = QUERY_HEADS * HEAD_SIZE
    key_columns = KEY_VALUE_HEADS * HEAD_SIZE
    for layer_index in range(TEACHER_LAYERS):
        normed = rms_normed(hidden, attn_gain[layer_index])
        stacked = jnp.concatenate((w_query[layer_index], key_projection[layer_index], value_projection[layer_index]), axis=1)
        packed = jnp.dot(normed, stacked, preferred_element_type=jnp.float32).astype(jnp.bfloat16)
        blended = attend(packed, query_cols, key_columns)
        hidden = (hidden.astype(jnp.float32) + blocked_sum(blended, w_out[layer_index], N_TENSOR)).astype(jnp.bfloat16)
    student_out = blocked_sum(student_hidden, w_proj, N_TENSOR)
    residual_error = student_out - hidden.astype(jnp.float32)
    distill_loss = jnp.sum(residual_error * residual_error) / (2.0 * TOKENS * MODEL_WIDTH)
    error_rounded = residual_error.astype(jnp.bfloat16)
    proj_grad = lax.dot_general(student_hidden, error_rounded, (((0,), (0,)), ((), ())), preferred_element_type=jnp.float32) / TOKENS
    student_grad = lax.dot_general(error_rounded, w_proj, (((1,), (1,)), ((), ())), preferred_element_type=jnp.float32)
    return (hidden, distill_loss, proj_grad, student_grad)
```

```python
import math

import jax
import jax.numpy as jnp
from jax import lax
from jax.experimental import pallas as pl
from jax.experimental.pallas import tpu as pltpu
from jax.sharding import PartitionSpec as P

MODEL_WIDTH = 16384
HEAD_SIZE = 128
BLOCK = 128
EPSILON = 1e-05
F32 = jnp.float32
BF16 = jnp.bfloat16

CORE = ("dp", [(i, i ^ 1) for i in range(16)])
ZHI = ("dp", [(i, i ^ 2) for i in range(16)])
Y_PAIR = ("dp", [(i, i ^ 4) for i in range(16)])
Y_FAR = ("dp", [(i, i ^ 8) for i in range(16)])
Y_UP = ("dp", [(i, (i + 4) % 16) for i in range(16)])
Y_DOWN = ("dp", [(i, (i - 4) % 16) for i in range(16)])
ZLO = ("tensor", [(t, t ^ 4) for t in range(8)])
X_UP = ("tensor", [(t, (t & 4) | ((t + 1) & 3)) for t in range(8)])
X_FAR = ("tensor", [(t, (t & 4) | ((t + 2) & 3)) for t in range(8)])
X_DOWN = ("tensor", [(t, (t & 4) | ((t - 1) & 3)) for t in range(8)])


def send(values, route):
    return lax.ppermute(values, route[0], route[1])


def matmul(left, right):
    return jnp.dot(left, right, preferred_element_type=F32)


def add(first, *others):
    total = first.astype(F32)
    for other in others:
        total = total + other.astype(F32)
    return total

VMEM_LIMIT = 56 * 1024 * 1024
PLAIN = pltpu.CompilerParams(vmem_limit_bytes=VMEM_LIMIT)


def sum_everywhere(values):
    for route in (CORE, ZHI, Y_PAIR, Y_FAR):
        values = values + send(values, route)
    return values


def whole(body, shapes, *operands, flops=0, scalars=None):
    size = sum(a.size * a.dtype.itemsize for a in operands)
    size += sum(math.prod(s.shape) * s.dtype.itemsize for s in shapes)
    in_specs = [pl.BlockSpec(memory_space=pltpu.VMEM)] * len(operands)
    if scalars is not None:
        in_specs = [pl.BlockSpec(memory_space=pltpu.SMEM)] + in_specs
        operands = (scalars, *operands)
    return pl.pallas_call(
        body,
        in_specs=in_specs,
        out_specs=[pl.BlockSpec(memory_space=pltpu.VMEM)] * len(shapes),
        out_shape=list(shapes),
        compiler_params=PLAIN,
        cost_estimate=pl.CostEstimate(flops=flops, bytes_accessed=size, transcendentals=0),
    )(*operands)


def stack_rows(*pieces):
    def body(*refs):
        start = 0
        for ref in refs[:-1]:
            refs[-1][start : start + ref.shape[0]] = ref[...]
            start += ref.shape[0]

    shape = jax.ShapeDtypeStruct((sum(p.shape[0] for p in pieces), pieces[0].shape[1]), pieces[0].dtype)
    return whole(body, (shape,), *pieces)[0]


def half_block(place_ref, z_apart, x_apart):
    return (place_ref[3] ^ z_apart) * 4 + ((place_ref[4] + x_apart) & 3)


def products(place, left, right, orders, block_of):
    blocks = left.reshape(-1, BLOCK, left.shape[-1])

    def body(place_ref, left_ref, right_ref, *out_refs):
        for order, out_ref in zip(orders, out_refs):
            for i in range(0, len(order), 2):
                rows = [left_ref[block_of(place_ref, *which)] for which in order[i : i + 2]]
                product = matmul(jnp.concatenate(rows), right_ref[...])
                out_ref[i * BLOCK : (i + 2) * BLOCK] = product.astype(BF16)

    shapes = [jax.ShapeDtypeStruct((len(order) * BLOCK, right.shape[1]), BF16) for order in orders]
    flops = 2 * sum(len(order) for order in orders) * BLOCK * right.size
    return whole(body, shapes, blocks, right, flops=flops, scalars=place)


LEFT = 5 * HEAD_SIZE
RIGHT = 6 * HEAD_SIZE


def project_half(place, mine, hidden, gain, w_query, w_key, w_value, received=None):
    blocks = hidden.reshape(8, 2, BLOCK, hidden.shape[1])
    depth = hidden.shape[1]
    rows = 2 * BLOCK

    def body(place_ref, hidden_ref, gain_ref, query_ref, key_ref, value_ref, *refs):
        left_ref, right_ref = refs[-2:]
        values = hidden_ref[...].reshape(rows, depth).astype(F32)
        squares = jnp.sum(values * values, axis=1, keepdims=True)
        scaled = (values * gain_ref[...]).astype(BF16)
        left = matmul(scaled, query_ref[:, :LEFT])
        parts = [matmul(scaled, query_ref[:, LEFT:]), matmul(scaled, key_ref[...]), matmul(scaled, value_ref[...])]
        right = jnp.concatenate(parts, axis=1)
        if received is not None:
            left = left + refs[0][...].astype(F32)
            right = right + refs[1][:, :LEFT].astype(F32)
            squares = squares + jnp.sum(refs[1][:, LEFT:].astype(F32), axis=1, keepdims=True)
        left_ref[...] = left.astype(BF16)
        right_ref[:, :LEFT] = right.astype(BF16)
        high = squares.astype(BF16).astype(F32)
        middle = (squares - high).astype(BF16).astype(F32)
        low = squares - high - middle
        column = lax.broadcasted_iota(jnp.int32, (rows, HEAD_SIZE), 1)
        spread = jnp.where(column == 0, high, jnp.where(column == 1, middle, jnp.where(column == 2, low, 0.0)))
        right_ref[:, LEFT:] = spread.astype(BF16)

    def fixed(shape):
        return pl.BlockSpec(shape, lambda i, place_ref: (0,) * len(shape))

    in_specs = [
        pl.BlockSpec((2, 1, BLOCK, depth), lambda i, place_ref: (i, place_ref[2] if mine else 1 - place_ref[2], 0, 0)),
        fixed(gain.shape),
        fixed(w_query.shape),
        fixed(w_key.shape),
        fixed(w_value.shape),
    ]
    out_specs = [
        pl.BlockSpec((rows, LEFT), lambda i, place_ref: (i, 0)),
        pl.BlockSpec((rows, RIGHT), lambda i, place_ref: (i, 0)),
    ]
    operands = [blocks, gain, w_query, w_key, w_value]
    if received is not None:
        in_specs += out_specs
        operands += received
    return pl.pallas_call(
        body,
        grid_spec=pltpu.PrefetchScalarGridSpec(
            num_scalar_prefetch=1, grid=(4,), in_specs=in_specs, out_specs=out_specs
        ),
        out_shape=[jax.ShapeDtypeStruct((8 * BLOCK, n), BF16) for n in (LEFT, RIGHT)],
        compiler_params=PLAIN,
        cost_estimate=pl.CostEstimate(
            flops=2 * 8 * BLOCK * depth * 2 * LEFT, bytes_accessed=10 * 1024 * 1024, transcendentals=0
        ),
    )(place, *operands)


def sum_projections(left, right):
    def body(left_ref, right_ref, queries_ref, kv_ref):
        left_sum = left_ref[0].astype(F32)
        right_sum = right_ref[0].astype(F32)
        for i in range(1, 8):
            left_sum = left_sum + left_ref[i].astype(F32)
            right_sum = right_sum + right_ref[i].astype(F32)
        squares = jnp.sum(right_sum[:, LEFT:], axis=1, keepdims=True)
        scale = lax.rsqrt(squares / MODEL_WIDTH + EPSILON)
        queries_ref[:, :LEFT] = (left_sum * scale).astype(BF16)
        rest = (right_sum[:, :LEFT] * scale).astype(BF16)
        queries_ref[:, LEFT:] = rest[:, : 3 * HEAD_SIZE]
        for i in range(8):
            kv_ref[i] = rest[:, 3 * HEAD_SIZE :]

    return whole(
        body,
        (
            jax.ShapeDtypeStruct((BLOCK, 8 * HEAD_SIZE), BF16),
            jax.ShapeDtypeStruct((8, BLOCK, 2 * HEAD_SIZE), BF16),
        ),
        left,
        right,
    )


def attend(place, queries, kv_own, kv_other):
    heads = queries.shape[1] // HEAD_SIZE
    half = kv_own.shape[0] * BLOCK

    def body(place_ref, queries_ref, own_ref, other_ref, out_ref):
        block = place_ref[0] * 4 + place_ref[1] * 2 + place_ref[2]
        row = block * BLOCK + lax.broadcasted_iota(jnp.int32, (BLOCK, half), 0)
        column = lax.broadcasted_iota(jnp.int32, (BLOCK, half), 1)
        place = (column // BLOCK) * (2 * BLOCK) + column % BLOCK
        core = place_ref[2]
        own_kv = own_ref[...].reshape(half, 2 * HEAD_SIZE)
        other_kv = other_ref[...].reshape(half, 2 * HEAD_SIZE)
        sides = []
        for kv, parity in ((own_kv, core), (other_kv, 1 - core)):
            hidden = place + parity * BLOCK > row
            sides.append((kv[:, :HEAD_SIZE], kv[:, HEAD_SIZE:], hidden))
        for head in range(heads):
            span = slice(head * HEAD_SIZE, (head + 1) * HEAD_SIZE)
            query = queries_ref[:, span]
            scores = []
            for keys, _, hidden in sides:
                score = lax.dot_general(query, keys, (((1,), (1,)), ((), ())), preferred_element_type=F32)
                scores.append(jnp.where(hidden, -jnp.inf, score / math.sqrt(HEAD_SIZE)))
            top = jnp.maximum(*(jnp.max(s, axis=1, keepdims=True) for s in scores))
            weights = [jnp.exp(s - top) for s in scores]
            total = sum(jnp.sum(w, axis=1, keepdims=True) for w in weights)
            blended = sum(matmul(w.astype(BF16), side[1]) for w, side in zip(weights, sides))
            blended = (blended / total).astype(BF16)
            for i in range(8):
                out_ref[i, :, span] = blended

    shape = jax.ShapeDtypeStruct((8, BLOCK, heads * HEAD_SIZE), BF16)
    return whole(body, (shape,), queries, kv_own, kv_other, flops=2 ** 30, scalars=place)[0]


def split_for_ring(kept, received):
    count, width = kept.shape[0] // 4, kept.shape[1]
    half = count // 2

    def body(kept_ref, received_ref, up_ref, down_ref, rest_ref):
        total = (kept_ref[...].astype(F32) + received_ref[...].astype(F32)).astype(BF16)
        own, following, opposite, previous = (total[i * count : (i + 1) * count] for i in range(4))
        up_ref[:half] = opposite[:half]
        up_ref[half:] = following[half:]
        down_ref[:half] = opposite[half:]
        down_ref[half:] = previous[:half]
        rest_ref[:half] = following[:half]
        rest_ref[half : 2 * half] = previous[half:]
        rest_ref[2 * half :] = own

    return whole(
        body,
        [jax.ShapeDtypeStruct((n, width), BF16) for n in (count, count, 2 * count)],
        kept,
        received,
    )


def ring_scatter(up_part, down_part, rest, up, down):
    half = up_part.shape[0] // 2
    from_prev = send(up_part, up)
    from_next = send(down_part, down)
    low = send(add(rest[:half], from_prev[:half]).astype(BF16), up)
    high = send(add(rest[half : 2 * half], from_next[:half]).astype(BF16), down)
    return (
        add(rest[2 * half : 3 * half], from_next[half:], low),
        add(rest[3 * half :], from_prev[half:], high),
    )


def gather_of_four(own, up, down):
    half = own.shape[0] // 2
    previous = send(own, up)
    following = send(own, down)
    low = send(previous[:half], up)
    high = send(following[half:], down)
    return own, following, low, high, previous


ORDERS_Z = [[(1, 0), (1, 1), (1, 2), (1, 3)], [(0, 0), (0, 1), (0, 2), (0, 3)]]
ORDERS_X = [[(0, 2), (1, 1)], [(1, 2), (0, 3)], [(0, 1), (1, 3), (0, 0), (1, 0)]]


def error_half(place, mine, teacher, student, w_proj):
    depth, width = w_proj.shape

    def body(place_ref, teacher_ref, *refs):
        student_refs, (weight_ref, out_ref, error_ref, product_ref, squares_ref) = refs[:-5], refs[-5:]
        core = place_ref[2]
        parity = core if mine else 1 - core
        for k in range(8):
            dz, dx = place_ref[3] ^ (k // 4), (k - place_ref[4]) & 3
            block = teacher_ref[dx * 2 + dz if mine else dz * 4 + dx]
            out_ref[k] = block
            other = student_refs[0][dx * 4 + dz * 2 + parity]
            error = other.astype(F32) - block.astype(F32)
            error_ref[k] = error.astype(BF16)
            squares = jnp.sum((error * error).reshape(BLOCK // 8, 8, width), axis=0)
            squares_ref[...] = squares if k == 0 else squares_ref[...] + squares
        for k in range(0, 8, 2):
            errors = error_ref[k : k + 2].reshape(2 * BLOCK, width)
            product = lax.dot_general(
                errors, weight_ref[...], (((1,), (1,)), ((), ())), preferred_element_type=F32
            )
            product_ref[k : k + 2] = product.astype(BF16).reshape(2, BLOCK, depth)

    half = jax.ShapeDtypeStruct((8, BLOCK, width), BF16)
    return whole(
        body,
        (half, half, jax.ShapeDtypeStruct((8, BLOCK, depth), BF16), jax.ShapeDtypeStruct((8, width), F32)),
        teacher.reshape(8, BLOCK, width),
        student.reshape(16, BLOCK, width),
        w_proj,
        flops=2 * 8 * BLOCK * width * depth,
        scalars=place,
    )


def interleave(place, own, other):
    def body(place_ref, own_ref, other_ref, out_ref):
        core = place_ref[2]
        for k in range(8):
            out_ref[2 * k + core] = own_ref[k]
            out_ref[2 * k + 1 - core] = other_ref[k]

    shape = jax.ShapeDtypeStruct((16, *own.shape[1:]), own.dtype)
    return whole(body, (shape,), own, other, scalars=place)[0]


def split_grads(place, kept, received):
    width = kept.shape[2]

    def body(place_ref, kept_ref, received_ref, up_ref, down_ref, rest_ref):
        def block(y_apart, z_apart):
            k = ((place_ref[0] + y_apart) & 3) * 2 + (place_ref[1] ^ z_apart)
            return (kept_ref[k].astype(F32) + received_ref[k].astype(F32)).astype(BF16)

        up_ref[:BLOCK] = block(2, 0)
        up_ref[BLOCK:] = block(1, 1)
        down_ref[:BLOCK] = block(2, 1)
        down_ref[BLOCK:] = block(3, 0)
        for i, (dy, dz) in enumerate(((1, 0), (3, 1), (0, 0), (0, 1))):
            rest_ref[i * BLOCK : (i + 1) * BLOCK] = block(dy, dz)

    return whole(
        body,
        [jax.ShapeDtypeStruct((n * BLOCK, width), BF16) for n in (2, 2, 4)],
        kept,
        received,
        scalars=place,
    )


def over_chips(values):
    groups = [[2 * i + core for i in range(8)] for core in range(2)]
    return lax.all_to_all(values, "dp", 0, 0, axis_index_groups=groups)


def on_device(
    teacher_hidden, attn_gain, w_query, key_projection, value_projection, w_out, student_hidden, w_proj
):
    tokens, width = teacher_hidden.shape
    dp = lax.axis_index("dp")
    tensor = lax.axis_index("tensor")
    core = dp % 2
    place = jnp.stack([dp // 4, (dp // 2) % 2, core, tensor // 4, tensor % 4])

    weights = (attn_gain, w_query[0], key_projection[0], value_projection[0])
    sent = project_half(place, False, teacher_hidden, *weights)
    received = [send(part, CORE) for part in sent]

    orders = [[(dx, dz, parity) for dz in range(2) for parity in range(2)] for dx in range(4)]
    student_parts = products(
        place, student_hidden, w_proj, orders, lambda ref, dx, dz, parity: 2 * half_block(ref, dz, dx) + parity
    )
    student_parts, received = lax.optimization_barrier((student_parts, received))
    student_far = send(student_parts[2], X_FAR)
    student_got = [send(student_parts[1], X_UP), send(student_parts[3], X_DOWN)]
    left, right = project_half(place, True, teacher_hidden, *weights, received=received)
    right = over_chips(right.reshape(8, BLOCK, RIGHT))
    left, student_far = lax.optimization_barrier((left, student_far))
    left = over_chips(left.reshape(8, BLOCK, LEFT))
    left, right, student_got = lax.optimization_barrier((left, right, student_got))
    queries, kv = sum_projections(left, right)

    student_row = add(student_parts[0], student_far, *student_got).astype(BF16)
    student_zlo = send(student_row[2 * BLOCK :], ZLO)
    kv_own = over_chips(kv)
    kv_own, student_zlo = lax.optimization_barrier((kv_own, student_zlo))
    student_sum = add(student_row[: 2 * BLOCK], student_zlo).astype(BF16)
    student_other = send(student_sum, ZLO)
    kv_other = send(kv_own, CORE)
    blended = attend(place, queries, kv_own, kv_other)
    blended, student_other = lax.optimization_barrier((blended, student_other))
    student_pair = stack_rows(student_sum, student_other)
    student_prev, student_next = send(student_pair, X_UP), send(student_pair, X_DOWN)

    heads_own = over_chips(blended)
    heads_own, student_prev, student_next = lax.optimization_barrier((heads_own, student_prev, student_next))
    heads_other = send(heads_own, CORE)
    student_low = send(student_prev[: 2 * BLOCK], X_UP)
    student_high = send(student_next[2 * BLOCK :], X_DOWN)
    out_weight = w_out[0]
    z_sent, z_kept = products(place, heads_own, out_weight, ORDERS_Z, half_block)
    z_sent = send(z_sent, ZLO)
    z_sent, student_low, student_high = lax.optimization_barrier((z_sent, student_low, student_high))
    low, high = ring_scatter(*products(place, heads_other, out_weight, ORDERS_X, half_block), X_UP, X_DOWN)
    other_z = send(high.astype(BF16), ZLO)
    low_own, high_own = ring_scatter(*split_for_ring(z_kept, z_sent), X_UP, X_DOWN)

    def hidden_block(parity):
        return lax.dynamic_slice_in_dim(teacher_hidden, (2 * tensor + parity) * BLOCK, BLOCK).astype(F32)

    teacher_other = (hidden_block(1 - core) + low + other_z.astype(F32)).astype(BF16)
    teacher_own = (hidden_block(core) + jnp.concatenate((low_own, high_own))).astype(BF16)

    other_row = stack_rows(*gather_of_four(teacher_other, X_UP, X_DOWN))
    teacher_other = stack_rows(other_row, send(other_row, ZLO))
    own_pair = stack_rows(teacher_own, send(teacher_own, ZLO))
    teacher_own = stack_rows(*gather_of_four(own_pair, X_UP, X_DOWN))

    student = stack_rows(student_pair, student_next, student_low, student_high, student_prev)
    out_other, error_other, grad_other, squares_other = error_half(place, False, teacher_other, student, w_proj)
    grad_other = send(grad_other, CORE)
    out_own, error_own, grad_own, squares_own = error_half(place, True, teacher_own, student, w_proj)
    loss_part = jnp.sum(squares_other + squares_own)
    low, high = ring_scatter(*split_grads(place, grad_own, grad_other), Y_UP, Y_DOWN)
    student_grad = low + send(high.astype(BF16), ZHI).astype(F32)
    distill_loss = sum_everywhere(loss_part) / (2.0 * tokens * MODEL_WIDTH)
    teacher_out = interleave(place, out_own, out_other).reshape(tokens, width)
    rows = student_hidden.reshape(8, 2, BLOCK, -1)
    proj_grad = 0.0
    for errors, parity in ((error_other, 1 - core), (error_own, core)):
        half = lax.dynamic_index_in_dim(rows, parity, 1, keepdims=False).reshape(8 * BLOCK, -1)
        proj_grad = proj_grad + lax.dot_general(
            half, errors.reshape(8 * BLOCK, width), (((0,), (0,)), ((), ())), preferred_element_type=F32
        )
    return (teacher_out, distill_loss, proj_grad / tokens, student_grad)


def solution(mesh):
    return jax.shard_map(
        on_device,
        mesh=mesh,
        in_specs=(
            P(None, "dp"),
            P(None, "dp"),
            P(None, "dp", "tensor"),
            P(None, "dp", "tensor"),
            P(None, "dp", "tensor"),
            P(None, "tensor", "dp"),
            P(None, "tensor"),
            P("tensor", "dp"),
        ),
        out_specs=(P(None, "dp"), P(), P("tensor", "dp"), P("dp", "tensor")),
        check_vma=False,
    )
```

```python
import math

import jax
import jax.numpy as jnp
from jax import lax
from jax.experimental import pallas as pl
from jax.experimental.pallas import tpu as pltpu
from jax.sharding import PartitionSpec as P

MODEL_WIDTH = 16384
HEAD_SIZE = 128
BLOCK = 128
EPSILON = 1e-05
F32 = jnp.float32
BF16 = jnp.bfloat16

CORE = ("dp", [(i, i ^ 1) for i in range(16)])
ZHI = ("dp", [(i, i ^ 2) for i in range(16)])
Y_FAR = ("dp", [(i, i ^ 8) for i in range(16)])
Y_UP = ("dp", [(i, (i + 4) % 16) for i in range(16)])
Y_DOWN = ("dp", [(i, (i - 4) % 16) for i in range(16)])
ZLO = ("tensor", [(t, t ^ 4) for t in range(8)])
CHIPS = [(dy, dz) for dy in range(4) for dz in range(2)]
TO_CHIP = {
    (dy, dz): ("dp", [(i, (i + 4 * dy) % 16 ^ (2 * dz)) for i in range(16)]) for dy, dz in CHIPS
}
X_UP = ("tensor", [(t, (t & 4) | ((t + 1) & 3)) for t in range(8)])
X_FAR = ("tensor", [(t, (t & 4) | ((t + 2) & 3)) for t in range(8)])
X_DOWN = ("tensor", [(t, (t & 4) | ((t - 1) & 3)) for t in range(8)])


def send(values, route):
    return lax.ppermute(values, route[0], route[1])


def matmul(left, right):
    return jnp.dot(left, right, preferred_element_type=F32)


def add(first, *others):
    total = first.astype(F32)
    for other in others:
        total = total + other.astype(F32)
    return total

VMEM_LIMIT = 56 * 1024 * 1024
PLAIN = pltpu.CompilerParams(vmem_limit_bytes=VMEM_LIMIT)


def whole(body, shapes, *operands, flops=0, scalars=None, scratch=()):
    size = sum(a.size * a.dtype.itemsize for a in operands)
    size += sum(math.prod(s.shape) * s.dtype.itemsize for s in shapes)
    in_specs = [pl.BlockSpec(memory_space=pltpu.VMEM)] * len(operands)
    if scalars is not None:
        in_specs = [pl.BlockSpec(memory_space=pltpu.SMEM)] + in_specs
        operands = (scalars, *operands)
    return pl.pallas_call(
        body,
        in_specs=in_specs,
        out_specs=[pl.BlockSpec(memory_space=pltpu.VMEM)] * len(shapes),
        out_shape=list(shapes),
        scratch_shapes=list(scratch),
        compiler_params=PLAIN,
        cost_estimate=pl.CostEstimate(flops=flops, bytes_accessed=size, transcendentals=0),
    )(*operands)


def stack_rows(*pieces):
    def body(*refs):
        start = 0
        for ref in refs[:-1]:
            refs[-1][start : start + ref.shape[0]] = ref[...]
            start += ref.shape[0]

    shape = jax.ShapeDtypeStruct((sum(p.shape[0] for p in pieces), pieces[0].shape[1]), pieces[0].dtype)
    return whole(body, (shape,), *pieces)[0]


def half_block(place_ref, z_apart, x_apart):
    return (place_ref[3] ^ z_apart) * 4 + ((place_ref[4] + x_apart) & 3)


def products(place, left, right, orders, unit, unit_of):
    units = left.reshape(-1, unit, left.shape[-1])
    group = 2 * BLOCK // unit

    def body(place_ref, left_ref, right_ref, *out_refs):
        for order, out_ref in zip(orders, out_refs):
            for i in range(0, len(order), group):
                rows = [left_ref[unit_of(place_ref, *which)] for which in order[i : i + group]]
                product = matmul(jnp.concatenate(rows), right_ref[...])
                out_ref[i * unit : (i + group) * unit] = product.astype(BF16)

    shapes = [jax.ShapeDtypeStruct((len(order) * unit, right.shape[1]), BF16) for order in orders]
    flops = 2 * sum(len(order) for order in orders) * unit * right.size
    return whole(body, shapes, units, right, flops=flops, scalars=place)


LEFT = 6 * HEAD_SIZE
KV = 2 * HEAD_SIZE
SUMS = 4 * HEAD_SIZE
RIGHT = 5 * HEAD_SIZE


def project(place, mine, on_left, hidden, gain, weights, received=None):
    blocks = hidden.reshape(8, 2, BLOCK, hidden.shape[1])
    depth = hidden.shape[1]
    rows = 2 * BLOCK
    columns = LEFT if on_left else RIGHT
    n_weights = len(weights)

    def body(place_ref, hidden_ref, gain_ref, *refs):
        out_ref = refs[-1]
        values = hidden_ref[...].reshape(rows, depth).astype(F32)
        scaled = (values * gain_ref[...]).astype(BF16)
        parts = [ref[...] for ref in refs[:n_weights]]
        if not on_left:
            parts = [parts[0], jnp.concatenate(parts[1:], axis=1)]
        product = jnp.concatenate([matmul(scaled, part) for part in parts], axis=1)
        width = product.shape[1]
        if received is not None:
            got_ref = refs[n_weights]
            product = product + got_ref[:, :width].astype(F32)
        out_ref[:, :width] = product.astype(BF16)
        if on_left:
            return
        squares = jnp.sum(values * values, axis=1, keepdims=True)
        if received is not None:
            squares = squares + jnp.sum(got_ref[:, SUMS:].astype(F32), axis=1, keepdims=True)
        high = squares.astype(BF16).astype(F32)
        middle = (squares - high).astype(BF16).astype(F32)
        low = squares - high - middle
        column = lax.broadcasted_iota(jnp.int32, (rows, HEAD_SIZE), 1)
        spread = jnp.where(column == 0, high, jnp.where(column == 1, middle, jnp.where(column == 2, low, 0.0)))
        out_ref[:, SUMS:] = spread.astype(BF16)

    def fixed(shape, column=0):
        return pl.BlockSpec(shape, lambda i, place_ref: (0, column))

    query_spec = fixed((depth, LEFT)) if on_left else fixed((depth, KV), LEFT // KV)
    in_specs = [
        pl.BlockSpec((2, 1, BLOCK, depth), lambda i, place_ref: (i, place_ref[2] if mine else 1 - place_ref[2], 0, 0)),
        fixed(gain.shape),
        query_spec,
        *(fixed(w.shape) for w in weights[1:]),
    ]
    out_spec = pl.BlockSpec((rows, columns), lambda i, place_ref: (i, 0))
    operands = [blocks, gain, *weights]
    if received is not None:
        in_specs.append(out_spec)
        operands.append(received)
    return pl.pallas_call(
        body,
        grid_spec=pltpu.PrefetchScalarGridSpec(
            num_scalar_prefetch=1, grid=(4,), in_specs=in_specs, out_specs=out_spec
        ),
        out_shape=jax.ShapeDtypeStruct((8 * BLOCK, columns), BF16),
        compiler_params=PLAIN,
        cost_estimate=pl.CostEstimate(
            flops=2 * 8 * BLOCK * depth * columns, bytes_accessed=6 * 1024 * 1024, transcendentals=0
        ),
    )(place, *operands)


def sum_right(right):
    def body(right_ref, scale_ref, queries_ref, kv_ref):
        total = right_ref[0].astype(F32)
        for i in range(1, 8):
            total = total + right_ref[i].astype(F32)
        squares = jnp.sum(total[:, SUMS:], axis=1, keepdims=True)
        scale = lax.rsqrt(squares / MODEL_WIDTH + EPSILON)
        scale_ref[...] = jnp.broadcast_to(scale, (BLOCK, HEAD_SIZE))
        queries_ref[...] = (total[:, :KV] * scale).astype(BF16)
        kv_ref[...] = (total[:, KV:SUMS] * scale).astype(BF16)

    shapes = [jax.ShapeDtypeStruct((BLOCK, HEAD_SIZE), F32), *[jax.ShapeDtypeStruct((BLOCK, KV), BF16)] * 2]
    return whole(body, shapes, right)


def attend(place, left, scale, queries_right, kv_own, kv_other):
    heads = LEFT // HEAD_SIZE + queries_right.shape[1] // HEAD_SIZE
    half = kv_own.shape[0]

    def body(place_ref, left_ref, scale_ref, right_ref, own_ref, other_ref, out_ref):
        y, z_hi, core = place_ref[0], place_ref[1], place_ref[2]
        row = (y * 4 + z_hi * 2 + core) * BLOCK + lax.broadcasted_iota(jnp.int32, (BLOCK, half), 0)
        column = lax.broadcasted_iota(jnp.int32, (BLOCK, half), 1)
        chip = column // BLOCK
        chip = ((chip // 2 + y) & 3) * 2 + (chip % 2 ^ z_hi)
        spot = chip * (2 * BLOCK) + column % BLOCK
        left_sum = left_ref[0].astype(F32)
        for i in range(1, 8):
            left_sum = left_sum + left_ref[i].astype(F32)
        left_queries = (left_sum * scale_ref[:, :1]).astype(BF16)
        sides = []
        for ref, parity in ((own_ref, core), (other_ref, 1 - core)):
            sides.append((ref[:, :HEAD_SIZE], ref[:, HEAD_SIZE:], spot + parity * BLOCK > row))
        for head in range(heads):
            span = slice(head * HEAD_SIZE, (head + 1) * HEAD_SIZE)
            if head * HEAD_SIZE < LEFT:
                query = left_queries[:, span]
            else:
                query = right_ref[:, head * HEAD_SIZE - LEFT : (head + 1) * HEAD_SIZE - LEFT]
            scores = []
            for keys, _, hidden in sides:
                score = lax.dot_general(query, keys, (((1,), (1,)), ((), ())), preferred_element_type=F32)
                scores.append(jnp.where(hidden, -jnp.inf, score / math.sqrt(HEAD_SIZE)))
            top = jnp.maximum(*(jnp.max(s, axis=1, keepdims=True) for s in scores))
            weights = [jnp.exp(s - top) for s in scores]
            total = sum(jnp.sum(w, axis=1, keepdims=True) for w in weights)
            blended = sum(matmul(w.astype(BF16), side[1]) for w, side in zip(weights, sides))
            blended = (blended / total).astype(BF16)
            for i in range(8):
                out_ref[i, :, span] = blended

    shape = jax.ShapeDtypeStruct((8, BLOCK, heads * HEAD_SIZE), BF16)
    operands = (left, scale, queries_right, kv_own, kv_other)
    return whole(body, (shape,), *operands, flops=2 ** 30, scalars=place)[0]


def ring_middle(rest, from_prev, from_next):
    half = from_prev.shape[0] // 2
    return add(rest[:half], from_prev[:half]).astype(BF16), add(rest[half : 2 * half], from_next[:half]).astype(BF16)


def ring_end(rest, from_prev, from_next, low, high):
    half = from_prev.shape[0] // 2
    return (
        add(rest[2 * half : 3 * half], from_next[half:], low),
        add(rest[3 * half :], from_prev[half:], high),
    )


HALF_BLOCK = BLOCK // 2
UP_DOWN = [(2, 0), (1, 1), (2, 1), (3, 0)]
REST = [(1, 0), (3, 1), (0, 0), (0, 1)]
ORDERS_Z = [[(dz, dx, row) for dx, row in part] for dz in (1, 0) for part in (UP_DOWN, REST)]
ORDERS_X = [[(dz, dx) for dx, dz in part] for part in (UP_DOWN[:2], UP_DOWN[2:], REST)]
ORDERS_STUDENT = [[(dx, dz, parity) for parity in range(2)] for dx, dz in ((2, 0), (2, 1), (1, 1), (3, 0))]
ORDERS_STUDENT.append([(dx, dz, parity) for dx, dz in REST for parity in range(2)])


def error_half(place, mine, teacher, student, w_proj, carried=None):
    depth, width = w_proj.shape
    n_teacher = len(teacher)

    def body(place_ref, *refs):
        teacher_refs, student_refs = refs[:n_teacher], refs[n_teacher : n_teacher + 5]
        weight_ref = refs[n_teacher + 5]
        out_ref, error_ref, product_ref, squares_ref, parts_ref, sems = refs[-6:]
        parity = place_ref[2] if mine else 1 - place_ref[2]

        def part(pieces, z_apart, x_apart, rows):
            if x_apart == 2:
                return pieces[2 + z_apart], 0
            return pieces[(0, 1, 0, 4)[x_apart]], z_apart * rows

        copies = []
        for dz in range(2):
            for dx in range(4):
                k = half_block(place_ref, dz, dx)
                if mine:
                    ref, start = part(teacher_refs, dz, dx, BLOCK)
                else:
                    ref, start = teacher_refs[dz], dx * BLOCK
                copy = pltpu.make_async_copy(
                    ref.at[pl.ds(start, BLOCK)], out_ref.at[2 * k + parity], sems.at[dz * 4 + dx]
                )
                copy.start()
                copies.append(copy)
                block = ref[start : start + BLOCK]
                ref, start = part(student_refs, dz, dx, 2 * BLOCK)
                student_block = ref[pl.ds(pl.multiple_of(start + parity * BLOCK, BLOCK), BLOCK)]
                error = student_block.astype(F32) - block.astype(F32)
                error_ref[k] = error.astype(BF16)
                parts_ref[k] = jnp.sum((error * error).reshape(BLOCK // 8, 8, width), axis=0)
        squares = parts_ref[0]
        for k in range(1, 8):
            squares = squares + parts_ref[k]
        squares_ref[...] = squares
        for k in range(0, 8, 2):
            errors = error_ref[k : k + 2].reshape(2 * BLOCK, width)
            product = lax.dot_general(
                errors, weight_ref[...], (((1,), (1,)), ((), ())), preferred_element_type=F32
            )
            product_ref[k : k + 2] = product.astype(BF16).reshape(2, BLOCK, depth)

        for copy in copies:
            copy.wait()

    vmem, anywhere = pl.BlockSpec(memory_space=pltpu.VMEM), pl.BlockSpec(memory_space=pl.ANY)
    operands = [*teacher, *student, w_proj]
    in_specs = [pl.BlockSpec(memory_space=pltpu.SMEM)] + [vmem] * len(operands)
    aliases = {}
    if carried is not None:
        aliases = {len(in_specs): 0}
        operands.append(carried)
        in_specs.append(anywhere)
    return pl.pallas_call(
        body,
        in_specs=in_specs,
        out_specs=[anywhere, vmem, vmem, vmem],
        out_shape=[
            jax.ShapeDtypeStruct((16, BLOCK, width), BF16),
            jax.ShapeDtypeStruct((8, BLOCK, width), BF16),
            jax.ShapeDtypeStruct((8, BLOCK, depth), BF16),
            jax.ShapeDtypeStruct((8, width), F32),
        ],
        scratch_shapes=[pltpu.VMEM((8, 8, width), F32), pltpu.SemaphoreType.DMA((8,))],
        input_output_aliases=aliases,
        compiler_params=PLAIN,
        cost_estimate=pl.CostEstimate(
            flops=2 * 8 * BLOCK * width * depth, bytes_accessed=12 * 1024 * 1024, transcendentals=0
        ),
    )(place, *operands)


def split_grads(place, kept, received):
    width = kept.shape[2]

    def body(place_ref, kept_ref, received_ref, up_ref, down_ref, rest_ref):
        def block(y_apart, z_apart):
            k = ((place_ref[0] + y_apart) & 3) * 2 + (place_ref[1] ^ z_apart)
            return (kept_ref[k].astype(F32) + received_ref[k].astype(F32)).astype(BF16)

        up_ref[:BLOCK] = block(2, 0)
        up_ref[BLOCK:] = block(1, 1)
        down_ref[:BLOCK] = block(2, 1)
        down_ref[BLOCK:] = block(3, 0)
        for i, (dy, dz) in enumerate(((1, 0), (3, 1), (0, 0), (0, 1))):
            rest_ref[i * BLOCK : (i + 1) * BLOCK] = block(dy, dz)

    return whole(
        body,
        [jax.ShapeDtypeStruct((n * BLOCK, width), BF16) for n in (2, 2, 4)],
        kept,
        received,
        scalars=place,
    )


def over_chips(values):
    groups = [[2 * i + core for i in range(8)] for core in range(2)]
    return lax.all_to_all(values, "dp", 0, 0, axis_index_groups=groups)


def on_device(
    teacher_hidden, attn_gain, w_query, key_projection, value_projection, w_out, student_hidden, w_proj
):
    tokens, width = teacher_hidden.shape
    dp = lax.axis_index("dp")
    tensor = lax.axis_index("tensor")
    core = dp % 2
    place = jnp.stack([dp // 4, (dp // 2) % 2, core, tensor // 4, tensor % 4])

    *student_sent, student_rest = products(
        place,
        student_hidden,
        w_proj,
        ORDERS_STUDENT,
        BLOCK,
        lambda ref, dx, dz, parity: 2 * half_block(ref, dz, dx) + parity,
    )
    unit = 2 * BLOCK
    student_up, student_down = send(student_sent[0], X_UP), send(student_sent[1], X_DOWN)

    weights = (w_query[0], key_projection[0], value_projection[0])
    right_sent = project(place, False, False, teacher_hidden, attn_gain, weights)
    right_got = send(right_sent, CORE)
    left_sent = project(place, False, True, teacher_hidden, attn_gain, weights[:1])
    left_got = send(left_sent, CORE)
    right = project(place, True, False, teacher_hidden, attn_gain, weights, right_got)
    right = over_chips(right.reshape(8, BLOCK, RIGHT))
    left = project(place, True, True, teacher_hidden, attn_gain, weights[:1], left_got)
    left, student_up, student_down = lax.optimization_barrier((left, student_up, student_down))
    student_low = send(add(student_rest[:unit], student_up).astype(BF16), X_UP)
    student_high = send(add(student_rest[unit : 2 * unit], student_down).astype(BF16), X_DOWN)
    right, student_low, student_high = lax.optimization_barrier((right, student_low, student_high))
    scale, queries_right, kv = sum_right(right)
    left = over_chips(left.reshape(8, BLOCK, LEFT))

    kv_blocks = [kv] + [send(kv, TO_CHIP[(-dy % 4, dz)]) for dy, dz in CHIPS[1:]]
    student_next, student_prev = send(student_sent[2], X_UP), send(student_sent[3], X_DOWN)
    left, kv_blocks, student_next, student_prev = lax.optimization_barrier(
        (left, kv_blocks, student_next, student_prev)
    )
    kv_own = stack_rows(*kv_blocks)
    kv_other = send(kv_own, CORE)
    student_row = add(student_rest[3 * unit :], student_high, student_next).astype(BF16)
    student_zlo = send(student_row, ZLO)
    kv_other, student_zlo = lax.optimization_barrier((kv_other, student_zlo))
    student_sum = add(student_rest[2 * unit : 3 * unit], student_low, student_prev, student_zlo).astype(BF16)
    student_other = send(student_sum, ZLO)
    blended = attend(place, left, scale, queries_right, kv_own, kv_other)
    blended, student_other = lax.optimization_barrier((blended, student_other))
    student_pair = stack_rows(student_sum, student_other)
    student_prev, student_next = send(student_pair, X_UP), send(student_pair, X_DOWN)

    heads_own = over_chips(blended)
    heads_own, student_prev, student_next = lax.optimization_barrier((heads_own, student_prev, student_next))
    heads_other = send(heads_own, CORE)
    student_low = send(student_prev[:unit], X_UP)
    student_high = send(student_next[unit:], X_DOWN)
    student = (student_pair, student_next, student_low, student_high, student_prev)
    out_weight = w_out[0]

    def half_of_block(ref, dz, dx, row):
        return 2 * half_block(ref, dz, dx) + row

    moved, moved_rest = products(place, heads_own, out_weight, ORDERS_Z[:2], HALF_BLOCK, half_of_block)
    moved, moved_rest = send(moved, ZLO), send(moved_rest, ZLO)
    up, down, other_rest = products(place, heads_other, out_weight, ORDERS_X, BLOCK, half_block)
    kept, kept_rest = products(place, heads_own, out_weight, ORDERS_Z[2:], HALF_BLOCK, half_of_block)
    other_prev, other_next = send(up, X_UP), send(down, X_DOWN)
    moved, kept, kept_rest = lax.optimization_barrier((moved, kept, kept_rest))
    up = add(kept[:BLOCK], moved[:BLOCK]).astype(BF16)
    down = add(kept[BLOCK:], moved[BLOCK:]).astype(BF16)
    up, down, other_prev, other_next = lax.optimization_barrier((up, down, other_prev, other_next))
    own_prev, own_next = send(up, X_UP), send(down, X_DOWN)
    low, high = ring_middle(other_rest, other_prev, other_next)
    moved_rest, low, high = lax.optimization_barrier((moved_rest, low, high))
    low, high = send(low, X_UP), send(high, X_DOWN)
    own_rest = add(kept_rest, moved_rest)
    own_low, own_high = ring_middle(own_rest, own_prev, own_next)
    own_low, own_high, low, high = lax.optimization_barrier((own_low, own_high, low, high))
    own_low, own_high = send(own_low, X_UP), send(own_high, X_DOWN)
    low, high = ring_end(other_rest, other_prev, other_next, low, high)
    high = send(high.astype(BF16), ZLO)
    high, own_low, own_high = lax.optimization_barrier((high, own_low, own_high))

    def hidden_block(parity):
        return lax.dynamic_slice_in_dim(teacher_hidden, (2 * tensor + parity) * BLOCK, BLOCK).astype(F32)

    other_block = (hidden_block(1 - core) + low + high.astype(F32)).astype(BF16)
    own_sum = jnp.concatenate(ring_end(own_rest, own_prev, own_next, own_low, own_high))
    own_block = (hidden_block(core) + own_sum).astype(BF16)

    other_prev, other_next = send(other_block, X_UP), send(other_block, X_DOWN)
    own_z = send(own_block, ZLO)
    own_z, other_prev, other_next = lax.optimization_barrier((own_z, other_prev, other_next))
    low, high = send(other_prev[: BLOCK // 2], X_UP), send(other_next[BLOCK // 2 :], X_DOWN)
    own_pair = stack_rows(own_block, own_z)
    own_prev, own_next = send(own_pair, X_UP), send(own_pair, X_DOWN)
    other_row = stack_rows(other_block, other_next, low, high, other_prev)
    other_row, own_prev, own_next = lax.optimization_barrier((other_row, own_prev, own_next))
    other_z = send(other_row, ZLO)
    own_low, own_high = send(own_prev[:BLOCK], X_UP), send(own_next[BLOCK:], X_DOWN)
    other_z, own_low, own_high = lax.optimization_barrier((other_z, own_low, own_high))
    teacher_other = (other_row, other_z)
    teacher_own = (own_pair, own_next, own_low, own_high, own_prev)

    teacher_out, error_other, grad_other, squares_other = error_half(place, False, teacher_other, student, w_proj)
    grad_other = send(grad_other, CORE)
    teacher_out, error_own, grad_own, squares_own = error_half(
        place, True, teacher_own, student, w_proj, teacher_out
    )
    loss = jnp.sum(squares_other + squares_own)
    up, down, rest = split_grads(place, grad_own, grad_other)
    from_prev, from_next, loss_core = send(up, Y_UP), send(down, Y_DOWN), send(loss, CORE)
    from_prev, from_next, loss_core = lax.optimization_barrier((from_prev, from_next, loss_core))
    loss = loss + loss_core
    low, high = ring_middle(rest, from_prev, from_next)
    low, high, loss_z = send(low, Y_UP), send(high, Y_DOWN), send(loss, ZHI)
    low, high, loss_z = lax.optimization_barrier((low, high, loss_z))
    loss = loss + loss_z
    low, high = ring_end(rest, from_prev, from_next, low, high)
    losses = [send(loss, route) for route in (Y_FAR, Y_UP, Y_DOWN)]
    high, *losses = lax.optimization_barrier((send(high.astype(BF16), ZHI), *losses))
    student_grad = low + high.astype(F32)
    distill_loss = ((loss + losses[0]) + (losses[1] + losses[2])) / (2.0 * tokens * MODEL_WIDTH)
    rows = student_hidden.reshape(8, 2, BLOCK, -1)
    proj_grad = 0.0
    for errors, parity in ((error_other, 1 - core), (error_own, core)):
        half = lax.dynamic_index_in_dim(rows, parity, 1, keepdims=False).reshape(8 * BLOCK, -1)
        proj_grad = proj_grad + lax.dot_general(
            half, errors.reshape(8 * BLOCK, width), (((0,), (0,)), ((), ())), preferred_element_type=F32
        )
    return (teacher_out.reshape(tokens, width), distill_loss, proj_grad / tokens, student_grad)


def solution(mesh):
    return jax.shard_map(
        on_device,
        mesh=mesh,
        in_specs=(
            P(None, "dp"),
            P(None, "dp"),
            P(None, "dp", "tensor"),
            P(None, "dp", "tensor"),
            P(None, "dp", "tensor"),
            P(None, "tensor", "dp"),
            P(None, "tensor"),
            P("tensor", "dp"),
        ),
        out_specs=(P(None, "dp"), P(), P("tensor", "dp"), P("dp", "tensor")),
        check_vma=False,
    )
```

```python
import math

import jax
import jax.numpy as jnp
from jax import lax
from jax.experimental import pallas as pl
from jax.experimental.pallas import tpu as pltpu
from jax.sharding import PartitionSpec as P

MODEL_WIDTH = 16384
HEAD_SIZE = 128
BLOCK = 128
EPSILON = 1e-05
F32 = jnp.float32
BF16 = jnp.bfloat16

CORE = ("dp", [(i, i ^ 1) for i in range(16)])
ZHI = ("dp", [(i, i ^ 2) for i in range(16)])
Y_FAR = ("dp", [(i, i ^ 8) for i in range(16)])
Y_UP = ("dp", [(i, (i + 4) % 16) for i in range(16)])
Y_DOWN = ("dp", [(i, (i - 4) % 16) for i in range(16)])
ZLO = ("tensor", [(t, t ^ 4) for t in range(8)])
CHIPS = [(dy, dz) for dy in range(4) for dz in range(2)]
TO_CHIP = {
    (dy, dz): ("dp", [(i, (i + 4 * dy) % 16 ^ (2 * dz)) for i in range(16)]) for dy, dz in CHIPS
}
X_UP = ("tensor", [(t, (t & 4) | ((t + 1) & 3)) for t in range(8)])
X_FAR = ("tensor", [(t, (t & 4) | ((t + 2) & 3)) for t in range(8)])
X_DOWN = ("tensor", [(t, (t & 4) | ((t - 1) & 3)) for t in range(8)])


def send(values, route):
    return lax.ppermute(values, route[0], route[1])


def matmul(left, right):
    return jnp.dot(left, right, preferred_element_type=F32)


def add(first, *others):
    total = first.astype(F32)
    for other in others:
        total = total + other.astype(F32)
    return total

VMEM_LIMIT = 56 * 1024 * 1024
PLAIN = pltpu.CompilerParams(vmem_limit_bytes=VMEM_LIMIT)


def whole(body, shapes, *operands, flops=0, scalars=None, scratch=()):
    size = sum(a.size * a.dtype.itemsize for a in operands)
    size += sum(math.prod(s.shape) * s.dtype.itemsize for s in shapes)
    in_specs = [pl.BlockSpec(memory_space=pltpu.VMEM)] * len(operands)
    if scalars is not None:
        in_specs = [pl.BlockSpec(memory_space=pltpu.SMEM)] + in_specs
        operands = (scalars, *operands)
    return pl.pallas_call(
        body,
        in_specs=in_specs,
        out_specs=[pl.BlockSpec(memory_space=pltpu.VMEM)] * len(shapes),
        out_shape=list(shapes),
        scratch_shapes=list(scratch),
        compiler_params=PLAIN,
        cost_estimate=pl.CostEstimate(flops=flops, bytes_accessed=size, transcendentals=0),
    )(*operands)


def stack_rows(*pieces):
    def body(*refs):
        start = 0
        for ref in refs[:-1]:
            refs[-1][start : start + ref.shape[0]] = ref[...]
            start += ref.shape[0]

    shape = jax.ShapeDtypeStruct((sum(p.shape[0] for p in pieces), pieces[0].shape[1]), pieces[0].dtype)
    return whole(body, (shape,), *pieces)[0]


def half_block(place_ref, z_apart, x_apart):
    return (place_ref[3] ^ z_apart) * 4 + ((place_ref[4] + x_apart) & 3)


def products(place, left, right, orders, unit, unit_of):
    units = left.reshape(-1, unit, left.shape[-1])
    group = 2 * BLOCK // unit

    def body(place_ref, left_ref, right_ref, *out_refs):
        for order, out_ref in zip(orders, out_refs):
            for i in range(0, len(order), group):
                rows = [left_ref[unit_of(place_ref, *which)] for which in order[i : i + group]]
                product = matmul(jnp.concatenate(rows), right_ref[...])
                out_ref[i * unit : (i + group) * unit] = product.astype(BF16)

    shapes = [jax.ShapeDtypeStruct((len(order) * unit, right.shape[1]), BF16) for order in orders]
    flops = 2 * sum(len(order) for order in orders) * unit * right.size
    return whole(body, shapes, units, right, flops=flops, scalars=place)


LEFT = 6 * HEAD_SIZE
KV = 2 * HEAD_SIZE
SUMS = 4 * HEAD_SIZE
RIGHT = 5 * HEAD_SIZE


def project(place, mine, on_left, hidden, gain, weights, received=None):
    blocks = hidden.reshape(8, 2, BLOCK, hidden.shape[1])
    depth = hidden.shape[1]
    rows = 4 * BLOCK
    columns = LEFT if on_left else RIGHT
    n_weights = len(weights)

    def body(place_ref, hidden_ref, gain_ref, *refs):
        out_ref = refs[-1]
        values = hidden_ref[...].reshape(rows, depth).astype(F32)
        scaled = (values * gain_ref[...]).astype(BF16)
        parts = [ref[...] for ref in refs[:n_weights]]
        if not on_left:
            parts = [parts[0], jnp.concatenate(parts[1:], axis=1)]
        product = jnp.concatenate([matmul(scaled, part) for part in parts], axis=1)
        width = product.shape[1]
        if received is not None:
            got_ref = refs[n_weights]
            product = product + got_ref[:, :width].astype(F32)
        out_ref[:, :width] = product.astype(BF16)
        if on_left:
            return
        squares = jnp.sum(values * values, axis=1, keepdims=True)
        if received is not None:
            squares = squares + jnp.sum(got_ref[:, SUMS:].astype(F32), axis=1, keepdims=True)
        high = squares.astype(BF16).astype(F32)
        middle = (squares - high).astype(BF16).astype(F32)
        low = squares - high - middle
        column = lax.broadcasted_iota(jnp.int32, (rows, HEAD_SIZE), 1)
        spread = jnp.where(column == 0, high, jnp.where(column == 1, middle, jnp.where(column == 2, low, 0.0)))
        out_ref[:, SUMS:] = spread.astype(BF16)

    def fixed(shape, column=0):
        return pl.BlockSpec(shape, lambda i, place_ref: (0, column))

    query_spec = fixed((depth, LEFT)) if on_left else fixed((depth, KV), LEFT // KV)
    in_specs = [
        pl.BlockSpec((4, 1, BLOCK, depth), lambda i, place_ref: (i, place_ref[2] if mine else 1 - place_ref[2], 0, 0)),
        fixed(gain.shape),
        query_spec,
        *(fixed(w.shape) for w in weights[1:]),
    ]
    out_spec = pl.BlockSpec((rows, columns), lambda i, place_ref: (i, 0))
    operands = [blocks, gain, *weights]
    if received is not None:
        in_specs.append(out_spec)
        operands.append(received)
    return pl.pallas_call(
        body,
        grid_spec=pltpu.PrefetchScalarGridSpec(
            num_scalar_prefetch=1, grid=(2,), in_specs=in_specs, out_specs=out_spec
        ),
        out_shape=jax.ShapeDtypeStruct((8 * BLOCK, columns), BF16),
        compiler_params=PLAIN,
        cost_estimate=pl.CostEstimate(
            flops=2 * 8 * BLOCK * depth * columns, bytes_accessed=6 * 1024 * 1024, transcendentals=0
        ),
    )(place, *operands)


def sum_right(right):
    def body(right_ref, scale_ref, queries_ref, kv_ref):
        total = right_ref[0].astype(F32)
        for i in range(1, 8):
            total = total + right_ref[i].astype(F32)
        squares = jnp.sum(total[:, SUMS:], axis=1, keepdims=True)
        scale = lax.rsqrt(squares / MODEL_WIDTH + EPSILON)
        scale_ref[...] = jnp.broadcast_to(scale, (BLOCK, HEAD_SIZE))
        queries_ref[...] = (total[:, :KV] * scale).astype(BF16)
        kv_ref[...] = (total[:, KV:SUMS] * scale).astype(BF16)

    shapes = [jax.ShapeDtypeStruct((BLOCK, HEAD_SIZE), F32), *[jax.ShapeDtypeStruct((BLOCK, KV), BF16)] * 2]
    return whole(body, shapes, right)


def attend(place, left, scale, queries_right, kv_own, kv_other):
    heads = LEFT // HEAD_SIZE + queries_right.shape[1] // HEAD_SIZE
    half = kv_own.shape[0]

    def body(place_ref, left_ref, scale_ref, right_ref, own_ref, other_ref, out_ref):
        y, z_hi, core = place_ref[0], place_ref[1], place_ref[2]
        shape = (2 * BLOCK, half)
        row = (y * 4 + z_hi * 2 + core) * BLOCK + lax.broadcasted_iota(jnp.int32, shape, 0) % BLOCK
        column = lax.broadcasted_iota(jnp.int32, shape, 1)
        chip = column // BLOCK
        chip = ((chip // 2 + y) & 3) * 2 + (chip % 2 ^ z_hi)
        spot = chip * (2 * BLOCK) + column % BLOCK
        left_sum = left_ref[0].astype(F32)
        for i in range(1, 8):
            left_sum = left_sum + left_ref[i].astype(F32)
        left_queries = (left_sum * scale_ref[:, :1]).astype(BF16)
        sides = []
        for ref, parity in ((own_ref, core), (other_ref, 1 - core)):
            sides.append((ref[:, :HEAD_SIZE], ref[:, HEAD_SIZE:], spot + parity * BLOCK > row))
        for head in range(0, heads, 2):
            start = head * HEAD_SIZE
            pair = left_queries[:, start : start + KV] if start < LEFT else right_ref[...]
            query = jnp.concatenate((pair[:, :HEAD_SIZE], pair[:, HEAD_SIZE:]))
            scores = []
            for keys, _, hidden in sides:
                score = lax.dot_general(query, keys, (((1,), (1,)), ((), ())), preferred_element_type=F32)
                scores.append(jnp.where(hidden, -jnp.inf, score / math.sqrt(HEAD_SIZE)))
            top = jnp.maximum(*(jnp.max(s, axis=1, keepdims=True) for s in scores))
            weights = [jnp.exp(s - top) for s in scores]
            total = sum(jnp.sum(w, axis=1, keepdims=True) for w in weights)
            blended = sum(matmul(w.astype(BF16), side[1]) for w, side in zip(weights, sides))
            blended = (blended / total).astype(BF16)
            for i in range(8):
                out_ref[i, :, start : start + HEAD_SIZE] = blended[:BLOCK]
                out_ref[i, :, start + HEAD_SIZE : start + KV] = blended[BLOCK:]

    shape = jax.ShapeDtypeStruct((8, BLOCK, heads * HEAD_SIZE), BF16)
    operands = (left, scale, queries_right, kv_own, kv_other)
    return whole(body, (shape,), *operands, flops=2 ** 30, scalars=place)[0]


def add_far(following, previous, low, high):
    half = low.shape[0]

    def body(next_ref, previous_ref, low_ref, high_ref, up_ref, down_ref):
        up_ref[:half] = (next_ref[:half].astype(F32) + low_ref[...].astype(F32)).astype(BF16)
        up_ref[half:] = next_ref[half:]
        down_ref[:half] = previous_ref[:half]
        down_ref[half:] = (previous_ref[half:].astype(F32) + high_ref[...].astype(F32)).astype(BF16)

    shape = jax.ShapeDtypeStruct(following.shape, BF16)
    return whole(body, (shape, shape), following, previous, low, high)


def ring_middle(rest, from_prev, from_next):
    half = from_prev.shape[0] // 2
    return add(rest[:half], from_prev[:half]).astype(BF16), add(rest[half : 2 * half], from_next[:half]).astype(BF16)


def ring_end(rest, from_prev, from_next, low, high):
    half = from_prev.shape[0] // 2
    return (
        add(rest[2 * half : 3 * half], from_next[half:], low),
        add(rest[3 * half :], from_prev[half:], high),
    )


HALF_BLOCK = BLOCK // 2
UP_DOWN = [(2, 0), (1, 1), (2, 1), (3, 0)]
REST = [(1, 0), (3, 1), (0, 0), (0, 1)]
ORDERS_Z = [[(dz, dx, row) for dx, row in part] for dz in (1, 0) for part in (UP_DOWN, REST)]
ORDERS_X = [[(dz, dx) for dx, dz in part] for part in (UP_DOWN[:2], UP_DOWN[2:], REST)]
ORDERS_STUDENT = [
    [(dx, dz, parity) for dz in parts for parity in range(2)]
    for dx, parts in ((2, (0,)), (2, (1,)), (1, (0, 1)), (3, (0, 1)), (0, (0, 1)))
]


def error_blocks(place, groups, teacher, student, w_proj, carried=None):
    depth, width = w_proj.shape
    counts = [len(group) for group in groups]
    n_blocks, n_groups = sum(counts), len(groups)
    n_teacher, n_student = len(teacher), len(student)

    def body(place_ref, *refs):
        teacher_refs, student_refs = refs[:n_teacher], refs[n_teacher : n_teacher + n_student]
        weight_ref = refs[n_teacher + n_student]
        out_ref, error_ref, *product_refs = refs[-5 - n_groups : -3]
        squares_ref, scratch_ref, sems = refs[-3:]
        copies = []

        def start_copy(source, target):
            copy = pltpu.make_async_copy(source, target, sems.at[len(copies)])
            copy.start()
            copies.append(copy)

        i = 0
        for group, product_ref in zip(groups, product_refs):
            first = i
            for mine, dz, dx, piece, start in group:
                parity = place_ref[2] if mine else 1 - place_ref[2]
                block = 2 * half_block(place_ref, dz, dx) + parity
                source = teacher_refs[piece]
                start_copy(source.at[pl.ds(start, BLOCK)], out_ref.at[block])
                values = source[start : start + BLOCK].astype(F32)
                if dx == 2:
                    source, start = student_refs[2 + dz], 0
                else:
                    source, start = student_refs[(0, 1, 0, 4)[dx]], dz * 2 * BLOCK
                target = source[pl.ds(pl.multiple_of(start + parity * BLOCK, BLOCK), BLOCK)]
                error = target.astype(F32) - values
                scratch_ref[i] = error.astype(BF16)
                start_copy(scratch_ref.at[i], error_ref.at[block])
                squares_ref[i] = jnp.sum((error * error).reshape(BLOCK // 8, 8, width), axis=0)
                i += 1
            errors = scratch_ref[first:i].reshape((i - first) * BLOCK, width)
            product = lax.dot_general(
                errors, weight_ref[...], (((1,), (1,)), ((), ())), preferred_element_type=F32
            )
            product_ref[...] = product.astype(BF16)
        for copy in copies:
            copy.wait()

    vmem, anywhere = pl.BlockSpec(memory_space=pltpu.VMEM), pl.BlockSpec(memory_space=pl.ANY)
    operands = [*teacher, *student, w_proj]
    in_specs = [pl.BlockSpec(memory_space=pltpu.SMEM)] + [vmem] * len(operands)
    aliases = {}
    if carried is not None:
        aliases = {len(in_specs): 0, len(in_specs) + 1: 1}
        operands += carried
        in_specs += [anywhere] * 2
    return pl.pallas_call(
        body,
        in_specs=in_specs,
        out_specs=[anywhere] * 2 + [vmem] * (n_groups + 1),
        out_shape=[
            *[jax.ShapeDtypeStruct((16, BLOCK, width), BF16)] * 2,
            *[jax.ShapeDtypeStruct((count * BLOCK, depth), BF16) for count in counts],
            jax.ShapeDtypeStruct((n_blocks, 8, width), F32),
        ],
        scratch_shapes=[pltpu.VMEM((n_blocks, BLOCK, width), BF16), pltpu.SemaphoreType.DMA((2 * n_blocks,))],
        input_output_aliases=aliases,
        compiler_params=PLAIN,
        cost_estimate=pl.CostEstimate(
            flops=2 * n_blocks * BLOCK * width * depth, bytes_accessed=n_blocks * 2 ** 20, transcendentals=0
        ),
    )(place, *operands)


EARLY_OTHER = [(False, 0, 0, 0, 0), (False, 0, 1, 1, 0), (False, 0, 3, 2, 0)]
EARLY_OWN = [(True, dz, dx, piece, dz * BLOCK) for dx, piece in ((0, 3), (1, 4), (3, 5)) for dz in range(2)]
LATE_OTHER = [(False, 0, 2, 0, 0), (False, 1, 0, 1, 0), (False, 1, 1, 2, 0), (False, 1, 3, 2, BLOCK), (False, 1, 2, 3, 0)]
LATE_OWN = [(True, 0, 2, 0, 0), (True, 1, 2, 1, 0)]


def split_grads(place, own, other, squares):
    width = own[0].shape[1]
    early, late_other, late_own = squares

    def body(place_ref, *refs):
        own_refs, other_refs, square_refs = refs[:2], refs[2:4], refs[4:7]
        up_ref, down_ref, rest_ref, sum_ref, grads_ref, parts_ref = refs[7:]

        def places(blocks):
            return [half_block(place_ref, dz, dx) for _, dz, dx, _, _ in blocks]

        for refs_of, blocks, first in ((own_refs, (EARLY_OWN, LATE_OWN), True), (other_refs, (EARLY_OTHER, LATE_OTHER), False)):
            for ref, some in zip(refs_of, blocks):
                for i, k in enumerate(places(some)):
                    part = ref[i * BLOCK : (i + 1) * BLOCK].astype(F32)
                    grads_ref[k] = part if first else grads_ref[k] + part
        n_other = len(EARLY_OTHER)
        spots = [(square_refs[0], i, k) for i, k in enumerate(places(EARLY_OTHER))]
        spots += [(square_refs[0], n_other + i, 8 + k) for i, k in enumerate(places(EARLY_OWN))]
        spots += [(square_refs[1], i, k) for i, k in enumerate(places(LATE_OTHER))]
        spots += [(square_refs[2], i, 8 + k) for i, k in enumerate(places(LATE_OWN))]
        for ref, i, k in spots:
            parts_ref[k] = ref[i]
        total = parts_ref[0]
        for k in range(1, 16):
            total = total + parts_ref[k]
        sum_ref[...] = total

        def block(y_apart, z_apart):
            k = ((place_ref[0] + y_apart) & 3) * 2 + (place_ref[1] ^ z_apart)
            return grads_ref[k].astype(BF16)

        up_ref[:BLOCK] = block(2, 0)
        up_ref[BLOCK:] = block(1, 1)
        down_ref[:BLOCK] = block(2, 1)
        down_ref[BLOCK:] = block(3, 0)
        for i, (dy, dz) in enumerate(((1, 0), (3, 1), (0, 0), (0, 1))):
            rest_ref[i * BLOCK : (i + 1) * BLOCK] = block(dy, dz)

    return whole(
        body,
        [
            *[jax.ShapeDtypeStruct((n * BLOCK, width), BF16) for n in (2, 2, 4)],
            jax.ShapeDtypeStruct(early.shape[1:], F32),
        ],
        *own,
        *other,
        early,
        late_other,
        late_own,
        scalars=place,
        scratch=[pltpu.VMEM((8, BLOCK, width), F32), pltpu.VMEM((16, *early.shape[1:]), F32)],
    )


def over_chips(values):
    groups = [[2 * i + core for i in range(8)] for core in range(2)]
    return lax.all_to_all(values, "dp", 0, 0, axis_index_groups=groups)


def on_device(
    teacher_hidden, attn_gain, w_query, key_projection, value_projection, w_out, student_hidden, w_proj
):
    tokens, width = teacher_hidden.shape
    dp = lax.axis_index("dp")
    tensor = lax.axis_index("tensor")
    core = dp % 2
    place = jnp.stack([dp // 4, (dp // 2) % 2, core, tensor // 4, tensor % 4])

    *student_far, student_next, student_prev, student_own = products(
        place,
        student_hidden,
        w_proj,
        ORDERS_STUDENT,
        BLOCK,
        lambda ref, dx, dz, parity: 2 * half_block(ref, dz, dx) + parity,
    )
    unit = 2 * BLOCK
    student_up, student_down = send(student_far[0], X_UP), send(student_far[1], X_DOWN)

    weights = (w_query[0], key_projection[0], value_projection[0])
    right_sent = project(place, False, False, teacher_hidden, attn_gain, weights)
    right_got = send(right_sent, CORE)
    left_sent = project(place, False, True, teacher_hidden, attn_gain, weights[:1])
    left_got = send(left_sent, CORE)
    right = project(place, True, False, teacher_hidden, attn_gain, weights, right_got)
    right = over_chips(right.reshape(8, BLOCK, RIGHT))
    left = project(place, True, True, teacher_hidden, attn_gain, weights[:1], left_got)
    left, student_up, student_down = lax.optimization_barrier((left, student_up, student_down))
    student_next, student_prev = add_far(student_next, student_prev, student_up, student_down)
    student_up, student_down = send(student_next, X_UP), send(student_prev, X_DOWN)
    scale, queries_right, kv = sum_right(right)
    left = over_chips(left.reshape(8, BLOCK, LEFT))

    kv_blocks = [kv] + [send(kv, TO_CHIP[(-dy % 4, dz)]) for dy, dz in CHIPS[1:]]
    left, kv_blocks, student_up, student_down = lax.optimization_barrier((left, kv_blocks, student_up, student_down))
    kv_own = stack_rows(*kv_blocks)
    kv_other = send(kv_own, CORE)
    student_row = add(student_own[unit:], student_up[unit:], student_down[unit:]).astype(BF16)
    student_zlo = send(student_row, ZLO)
    kv_other, student_zlo = lax.optimization_barrier((kv_other, student_zlo))
    student_sum = add(student_own[:unit], student_up[:unit], student_down[:unit], student_zlo).astype(BF16)
    student_other = send(student_sum, ZLO)
    blended = attend(place, left, scale, queries_right, kv_own, kv_other)
    blended, student_other = lax.optimization_barrier((blended, student_other))
    student_pair = stack_rows(student_sum, student_other)
    student_prev, student_next = send(student_pair, X_UP), send(student_pair, X_DOWN)

    heads_own = over_chips(blended)
    heads_own, student_prev, student_next = lax.optimization_barrier((heads_own, student_prev, student_next))
    heads_other = send(heads_own, CORE)
    student_low = send(student_prev[:unit], X_UP)
    student_high = send(student_next[unit:], X_DOWN)
    out_weight = w_out[0]

    def half_of_block(ref, dz, dx, row):
        return 2 * half_block(ref, dz, dx) + row

    moved, moved_rest = products(place, heads_own, out_weight, ORDERS_Z[:2], HALF_BLOCK, half_of_block)
    moved, moved_rest = send(moved, ZLO), send(moved_rest, ZLO)
    up, down, other_rest = products(place, heads_other, out_weight, ORDERS_X, BLOCK, half_block)
    up, down, student_low, student_high = lax.optimization_barrier((up, down, student_low, student_high))
    kept, kept_rest = products(place, heads_own, out_weight, ORDERS_Z[2:], HALF_BLOCK, half_of_block)
    other_prev, other_next = send(up, X_UP), send(down, X_DOWN)
    moved, kept, kept_rest = lax.optimization_barrier((moved, kept, kept_rest))
    up = add(kept[:BLOCK], moved[:BLOCK]).astype(BF16)
    down = add(kept[BLOCK:], moved[BLOCK:]).astype(BF16)
    own_prev, own_next = send(up, X_UP), send(down, X_DOWN)
    low, high = ring_middle(other_rest, other_prev, other_next)
    low, high = send(low, X_UP), send(high, X_DOWN)
    own_rest = add(kept_rest, moved_rest)
    own_low, own_high = ring_middle(own_rest, own_prev, own_next)
    own_low, own_high, low, high = lax.optimization_barrier((own_low, own_high, low, high))
    own_low, own_high = send(own_low, X_UP), send(own_high, X_DOWN)
    low, high = ring_end(other_rest, other_prev, other_next, low, high)
    high = send(high.astype(BF16), ZLO)
    high, own_low, own_high = lax.optimization_barrier((high, own_low, own_high))

    def hidden_block(parity):
        return lax.dynamic_slice_in_dim(teacher_hidden, (2 * tensor + parity) * BLOCK, BLOCK).astype(F32)

    other_block = (hidden_block(1 - core) + low + high.astype(F32)).astype(BF16)
    own_sum = jnp.concatenate(ring_end(own_rest, own_prev, own_next, own_low, own_high))
    own_block = (hidden_block(core) + own_sum).astype(BF16)

    own_z, other_z = send(own_block, ZLO), send(other_block, ZLO)
    other_prev, other_next = send(other_block, X_UP), send(other_block, X_DOWN)
    own_z, other_prev, other_next = lax.optimization_barrier((own_z, other_prev, other_next))
    other_low, other_high = send(other_prev[:HALF_BLOCK], X_UP), send(other_next[HALF_BLOCK:], X_DOWN)
    own_pair = stack_rows(own_block, own_z)
    own_prev, own_next = send(own_pair, X_UP), send(own_pair, X_DOWN)
    other_sides = send(stack_rows(other_next, other_prev), ZLO)
    own_prev, own_next, other_low, other_high, other_sides = lax.optimization_barrier(
        (own_prev, own_next, other_low, other_high, other_sides)
    )
    other_far = stack_rows(other_low, other_high)
    other_far_z = send(other_far, ZLO)
    own_low, own_high = send(own_prev[:BLOCK], X_UP), send(own_next[BLOCK:], X_DOWN)

    student = (student_pair, student_next, student_low, student_high, student_prev)

    pieces = (other_block, other_next, other_prev, own_pair, own_next, own_prev)
    teacher_out, errors, early_other, early_own, early_squares = error_blocks(
        place, [EARLY_OTHER, EARLY_OWN], pieces, student, w_proj
    )
    early_other, other_far_z, own_low, own_high = lax.optimization_barrier(
        (early_other, other_far_z, own_low, own_high)
    )
    early_other = send(early_other, CORE)
    pieces = (other_far, other_z, other_sides, other_far_z)
    teacher_out, errors, late_other, other_squares = error_blocks(
        place, [LATE_OTHER], pieces, student, w_proj, (teacher_out, errors)
    )
    late_other = send(late_other, CORE)
    teacher_out, errors, late_own, own_squares = error_blocks(
        place, [LATE_OWN], (own_low, own_high), student, w_proj, (teacher_out, errors)
    )
    up, down, rest, squares = split_grads(
        place, (early_own, late_own), (early_other, late_other), (early_squares, other_squares, own_squares)
    )
    loss = jnp.sum(squares)
    proj_grad = lax.dot_general(
        student_hidden, errors.reshape(tokens, width), (((0,), (0,)), ((), ())), preferred_element_type=F32
    )
    proj_grad = proj_grad / tokens
    from_prev, from_next = send(up, Y_UP), send(down, Y_DOWN)
    losses = [send(loss, route) for route in (Y_FAR, Y_UP, Y_DOWN)]
    from_prev, from_next, *losses = lax.optimization_barrier((from_prev, from_next, *losses))
    loss = (loss + losses[0]) + (losses[1] + losses[2])
    low, high = ring_middle(rest, from_prev, from_next)
    low, high, loss_core = send(low, Y_UP), send(high, Y_DOWN), send(loss, CORE)
    low, high, loss_core, proj_grad = lax.optimization_barrier((low, high, loss_core, proj_grad))
    loss = loss + loss_core
    low, high = ring_end(rest, from_prev, from_next, low, high)
    high, loss_z = lax.optimization_barrier((send(high.astype(BF16), ZHI), send(loss, ZHI)))
    student_grad = low + high.astype(F32)
    distill_loss = (loss + loss_z) / (2.0 * tokens * MODEL_WIDTH)
    return (teacher_out.reshape(tokens, width), distill_loss, proj_grad, student_grad)


def solution(mesh):
    return jax.shard_map(
        on_device,
        mesh=mesh,
        in_specs=(
            P(None, "dp"),
            P(None, "dp"),
            P(None, "dp", "tensor"),
            P(None, "dp", "tensor"),
            P(None, "dp", "tensor"),
            P(None, "tensor", "dp"),
            P(None, "tensor"),
            P("tensor", "dp"),
        ),
        out_specs=(P(None, "dp"), P(), P("tensor", "dp"), P("dp", "tensor")),
        check_vma=False,
    )
```

```python
import math

import jax
import jax.numpy as jnp
from jax import lax
from jax.experimental import pallas as pl
from jax.experimental.pallas import tpu as pltpu
from jax.sharding import PartitionSpec as P

MODEL_WIDTH = 16384
HEAD_SIZE = 128
BLOCK = 128
EPSILON = 1e-05
F32 = jnp.float32
BF16 = jnp.bfloat16

CORE = ("dp", [(i, i ^ 1) for i in range(16)])
ZHI = ("dp", [(i, i ^ 2) for i in range(16)])
Y_FAR = ("dp", [(i, i ^ 8) for i in range(16)])
Y_UP = ("dp", [(i, (i + 4) % 16) for i in range(16)])
Y_DOWN = ("dp", [(i, (i - 4) % 16) for i in range(16)])
ZLO = ("tensor", [(t, t ^ 4) for t in range(8)])
CHIPS = [(dy, dz) for dy in range(4) for dz in range(2)]
TO_CHIP = {
    (dy, dz): ("dp", [(i, (i + 4 * dy) % 16 ^ (2 * dz)) for i in range(16)]) for dy, dz in CHIPS
}
X_UP = ("tensor", [(t, (t & 4) | ((t + 1) & 3)) for t in range(8)])
X_FAR = ("tensor", [(t, (t & 4) | ((t + 2) & 3)) for t in range(8)])
X_DOWN = ("tensor", [(t, (t & 4) | ((t - 1) & 3)) for t in range(8)])


def send(values, route):
    return lax.ppermute(values, route[0], route[1])


def matmul(left, right):
    return jnp.dot(left, right, preferred_element_type=F32)


def add(first, *others):
    total = first.astype(F32)
    for other in others:
        total = total + other.astype(F32)
    return total

VMEM_LIMIT = 56 * 1024 * 1024
PLAIN = pltpu.CompilerParams(vmem_limit_bytes=VMEM_LIMIT)


def whole(body, shapes, *operands, flops=0, scalars=None, scratch=()):
    size = sum(a.size * a.dtype.itemsize for a in operands)
    size += sum(math.prod(s.shape) * s.dtype.itemsize for s in shapes)
    in_specs = [pl.BlockSpec(memory_space=pltpu.VMEM)] * len(operands)
    if scalars is not None:
        in_specs = [pl.BlockSpec(memory_space=pltpu.SMEM)] + in_specs
        operands = (scalars, *operands)
    return pl.pallas_call(
        body,
        in_specs=in_specs,
        out_specs=[pl.BlockSpec(memory_space=pltpu.VMEM)] * len(shapes),
        out_shape=list(shapes),
        scratch_shapes=list(scratch),
        compiler_params=PLAIN,
        cost_estimate=pl.CostEstimate(flops=flops, bytes_accessed=size, transcendentals=0),
    )(*operands)


def stack_rows(*pieces):
    def body(*refs):
        start = 0
        for ref in refs[:-1]:
            refs[-1][start : start + ref.shape[0]] = ref[...]
            start += ref.shape[0]

    shape = jax.ShapeDtypeStruct((sum(p.shape[0] for p in pieces), pieces[0].shape[1]), pieces[0].dtype)
    return whole(body, (shape,), *pieces)[0]


def half_block(place_ref, z_apart, x_apart):
    return (place_ref[3] ^ z_apart) * 4 + ((place_ref[4] + x_apart) & 3)


def products(place, left, right, orders, unit, unit_of):
    units = left.reshape(-1, unit, left.shape[-1])

    def body(place_ref, left_ref, right_ref, *out_refs):
        rows = [left_ref[unit_of(place_ref, *which)] for order in orders for which in order]
        product = matmul(jnp.concatenate(rows), right_ref[...]).astype(BF16)
        start = 0
        for out_ref in out_refs:
            out_ref[...] = product[start : start + out_ref.shape[0]]
            start += out_ref.shape[0]

    shapes = [jax.ShapeDtypeStruct((len(order) * unit, right.shape[1]), BF16) for order in orders]
    flops = 2 * sum(len(order) for order in orders) * unit * right.size
    return whole(body, shapes, units, right, flops=flops, scalars=place)


LEFT = 6 * HEAD_SIZE
KV = 2 * HEAD_SIZE
SUMS = 4 * HEAD_SIZE
RIGHT = 5 * HEAD_SIZE


def project(place, mine, on_left, hidden, gain, weights, received=None):
    blocks = hidden.reshape(8, 2, BLOCK, hidden.shape[1])
    depth = hidden.shape[1]
    rows = 4 * BLOCK
    columns = LEFT if on_left else RIGHT
    n_weights = len(weights)

    def body(place_ref, hidden_ref, gain_ref, *refs):
        out_ref = refs[-1]
        values = hidden_ref[...].reshape(rows, depth).astype(F32)
        scaled = (values * gain_ref[...]).astype(BF16)
        parts = [ref[...] for ref in refs[:n_weights]]
        if not on_left:
            parts = [parts[0], jnp.concatenate(parts[1:], axis=1)]
        product = jnp.concatenate([matmul(scaled, part) for part in parts], axis=1)
        width = product.shape[1]
        if received is not None:
            got_ref = refs[n_weights]
            product = product + got_ref[:, :width].astype(F32)
        out_ref[:, :width] = product.astype(BF16)
        if on_left:
            return
        squares = jnp.sum(values * values, axis=1, keepdims=True)
        if received is not None:
            squares = squares + jnp.sum(got_ref[:, SUMS:].astype(F32), axis=1, keepdims=True)
        high = squares.astype(BF16).astype(F32)
        middle = (squares - high).astype(BF16).astype(F32)
        low = squares - high - middle
        column = lax.broadcasted_iota(jnp.int32, (rows, HEAD_SIZE), 1)
        spread = jnp.where(column == 0, high, jnp.where(column == 1, middle, jnp.where(column == 2, low, 0.0)))
        out_ref[:, SUMS:] = spread.astype(BF16)

    def fixed(shape, column=0):
        return pl.BlockSpec(shape, lambda i, place_ref: (0, column))

    query_spec = fixed((depth, LEFT)) if on_left else fixed((depth, KV), LEFT // KV)
    in_specs = [
        pl.BlockSpec((4, 1, BLOCK, depth), lambda i, place_ref: (i, place_ref[2] if mine else 1 - place_ref[2], 0, 0)),
        fixed(gain.shape),
        query_spec,
        *(fixed(w.shape) for w in weights[1:]),
    ]
    out_spec = pl.BlockSpec((rows, columns), lambda i, place_ref: (i, 0))
    operands = [blocks, gain, *weights]
    if received is not None:
        in_specs.append(out_spec)
        operands.append(received)
    return pl.pallas_call(
        body,
        grid_spec=pltpu.PrefetchScalarGridSpec(
            num_scalar_prefetch=1, grid=(2,), in_specs=in_specs, out_specs=out_spec
        ),
        out_shape=jax.ShapeDtypeStruct((8 * BLOCK, columns), BF16),
        compiler_params=PLAIN,
        cost_estimate=pl.CostEstimate(
            flops=2 * 8 * BLOCK * depth * columns, bytes_accessed=6 * 1024 * 1024, transcendentals=0
        ),
    )(place, *operands)


def sum_right(right, left):
    def body(right_ref, left_ref, scale_ref, queries_ref, both_ref):
        total = right_ref[0].astype(F32)
        for i in range(1, 8):
            total = total + right_ref[i].astype(F32)
        squares = jnp.sum(total[:, SUMS:], axis=1, keepdims=True)
        scale = lax.rsqrt(squares / MODEL_WIDTH + EPSILON)
        scale_ref[...] = jnp.broadcast_to(scale, (BLOCK, HEAD_SIZE))
        queries_ref[...] = (total[:, :KV] * scale).astype(BF16)
        key_value = (total[:, KV:SUMS] * scale).astype(BF16)
        both_ref[:, :, :LEFT] = left_ref[...]
        for i in range(8):
            both_ref[i, :, LEFT:] = key_value

    shapes = [
        jax.ShapeDtypeStruct((BLOCK, HEAD_SIZE), F32),
        jax.ShapeDtypeStruct((BLOCK, KV), BF16),
        jax.ShapeDtypeStruct((8, BLOCK, LEFT + KV), BF16),
    ]
    return whole(body, shapes, right, left)


def attend(place, both, scale, queries_right, kv_other):
    heads = LEFT // HEAD_SIZE + queries_right.shape[1] // HEAD_SIZE
    half = 8 * BLOCK

    def body(place_ref, both_ref, scale_ref, right_ref, other_ref, out_ref):
        y, z_hi, core = place_ref[0], place_ref[1], place_ref[2]
        shape = (2 * BLOCK, half)
        row = (y * 4 + z_hi * 2 + core) * BLOCK + lax.broadcasted_iota(jnp.int32, shape, 0) % BLOCK
        column = lax.broadcasted_iota(jnp.int32, shape, 1)
        spot = column // BLOCK * (2 * BLOCK) + column % BLOCK
        left_sum = both_ref[0, :, :LEFT].astype(F32)
        for i in range(1, 8):
            left_sum = left_sum + both_ref[i, :, :LEFT].astype(F32)
        left_queries = (left_sum * scale_ref[:, :1]).astype(BF16)
        sides = []
        own = both_ref[:, :, LEFT:].reshape(half, KV)
        other = other_ref[...].reshape(half, KV)
        for kv, parity in ((own, core), (other, 1 - core)):
            sides.append((kv[:, :HEAD_SIZE], kv[:, HEAD_SIZE:], spot + parity * BLOCK > row))
        for head in range(0, heads, 2):
            start = head * HEAD_SIZE
            pair = left_queries[:, start : start + KV] if start < LEFT else right_ref[...]
            query = jnp.concatenate((pair[:, :HEAD_SIZE], pair[:, HEAD_SIZE:]))
            scores = []
            for keys, _, hidden in sides:
                score = lax.dot_general(query, keys, (((1,), (1,)), ((), ())), preferred_element_type=F32)
                scores.append(jnp.where(hidden, -jnp.inf, score / math.sqrt(HEAD_SIZE)))
            top = jnp.maximum(*(jnp.max(s, axis=1, keepdims=True) for s in scores))
            weights = [jnp.exp(s - top) for s in scores]
            total = sum(jnp.sum(w, axis=1, keepdims=True) for w in weights)
            blended = sum(matmul(w.astype(BF16), side[1]) for w, side in zip(weights, sides))
            blended = (blended / total).astype(BF16)
            for i in range(8):
                out_ref[i, :, start : start + HEAD_SIZE] = blended[:BLOCK]
                out_ref[i, :, start + HEAD_SIZE : start + KV] = blended[BLOCK:]

    shape = jax.ShapeDtypeStruct((8, BLOCK, heads * HEAD_SIZE), BF16)
    operands = (both, scale, queries_right, kv_other)
    return whole(body, (shape,), *operands, flops=2 ** 30, scalars=place)[0]


def transposed(weight):
    def body(weight_ref, out_ref):
        out_ref[...] = weight_ref[...].T

    return whole(body, (jax.ShapeDtypeStruct(weight.shape[::-1], BF16),), weight)[0]


def add_far(following, previous, low, high):
    half = low.shape[0]

    def body(next_ref, previous_ref, low_ref, high_ref, up_ref, down_ref):
        up_ref[:half] = (next_ref[:half].astype(F32) + low_ref[...].astype(F32)).astype(BF16)
        up_ref[half:] = next_ref[half:]
        down_ref[:half] = previous_ref[:half]
        down_ref[half:] = (previous_ref[half:].astype(F32) + high_ref[...].astype(F32)).astype(BF16)

    shape = jax.ShapeDtypeStruct(following.shape, BF16)
    return whole(body, (shape, shape), following, previous, low, high)


def add_swapped(mine, theirs):
    half = mine.shape[0] // 2

    def body(mine_ref, theirs_ref, out_ref):
        out_ref[:half] = (mine_ref[:half].astype(F32) + theirs_ref[half:].astype(F32)).astype(BF16)
        out_ref[half:] = (mine_ref[half:].astype(F32) + theirs_ref[:half].astype(F32)).astype(BF16)

    return whole(body, (jax.ShapeDtypeStruct(mine.shape, BF16),), mine, theirs)[0]


def ring_middle(rest, from_prev, from_next):
    half = from_prev.shape[0] // 2
    return add(rest[:half], from_prev[:half]).astype(BF16), add(rest[half : 2 * half], from_next[:half]).astype(BF16)


def ring_end(rest, from_prev, from_next, low, high):
    half = from_prev.shape[0] // 2
    return (
        add(rest[2 * half : 3 * half], from_next[half:], low),
        add(rest[3 * half :], from_prev[half:], high),
    )


HALF_BLOCK = BLOCK // 2
UP_DOWN = [(2, 0), (1, 1), (2, 1), (3, 0)]
REST = [(1, 0), (3, 1), (0, 0), (0, 1)]
ORDERS_Z = [[(dz, dx, row) for dx, row in part] for dz in (1, 0) for part in (UP_DOWN, REST)]
ORDERS_X = [[(dz, dx) for dx, dz in part] for part in (UP_DOWN[:2], UP_DOWN[2:], REST)]
ORDERS_STUDENT = [
    [(dx, dz, parity) for dz in parts for parity in range(2)]
    for dx, parts in ((2, (0,)), (2, (1,)), (1, (0, 1)), (3, (0, 1)), (0, (0, 1)))
]
ORDERS_FAR, ORDERS_NEAR = ORDERS_STUDENT[:2], ORDERS_STUDENT[2:]


def error_blocks(place, groups, teacher, student, w_proj_t, carried=None):
    width, depth = w_proj_t.shape
    counts = [len(group) for group in groups]
    n_blocks, n_groups = sum(counts), len(groups)
    used = sorted({(dx, dz if dx == 2 else 0) for group in groups for _, dz, dx, _, _ in group})
    student = [student[(0, 1, 2 + dz, 4)[dx]] for dx, dz in used]
    n_teacher, n_student = len(teacher), len(student)

    def body(place_ref, *refs):
        teacher_refs, student_refs = refs[:n_teacher], refs[n_teacher : n_teacher + n_student]
        weight_ref = refs[n_teacher + n_student]
        out_ref, error_ref, *product_refs = refs[-5 - n_groups : -3]
        squares_ref, scratch_ref, sems = refs[-3:]
        copies = []

        def start_copy(source, target):
            copy = pltpu.make_async_copy(source, target, sems.at[len(copies)])
            copy.start()
            copies.append(copy)

        i = 0
        for group, product_ref in zip(groups, product_refs):
            first = i
            for mine, dz, dx, piece, start in group:
                parity = place_ref[2] if mine else 1 - place_ref[2]
                block = 2 * half_block(place_ref, dz, dx) + parity
                source = teacher_refs[piece]
                start_copy(source.at[pl.ds(start, BLOCK)], out_ref.at[block])
                values = source[start : start + BLOCK].astype(F32)
                if dx == 2:
                    source, start = student_refs[used.index((2, dz))], 0
                else:
                    source, start = student_refs[used.index((dx, 0))], dz * 2 * BLOCK
                target = source[pl.ds(pl.multiple_of(start + parity * BLOCK, BLOCK), BLOCK)]
                error = target.astype(F32) - values
                scratch_ref[i] = error.astype(BF16)
                start_copy(scratch_ref.at[i], error_ref.at[block])
                squares_ref[i] = jnp.sum((error * error).reshape(BLOCK // 8, 8, width), axis=0)
                i += 1
            errors = scratch_ref[first:i].reshape((i - first) * BLOCK, width)
            product_ref[...] = matmul(errors, weight_ref[...]).astype(BF16)
        for copy in copies:
            copy.wait()

    vmem, anywhere = pl.BlockSpec(memory_space=pltpu.VMEM), pl.BlockSpec(memory_space=pl.ANY)
    operands = [*teacher, *student, w_proj_t]
    in_specs = [pl.BlockSpec(memory_space=pltpu.SMEM)] + [vmem] * len(operands)
    aliases = {}
    if carried is not None:
        aliases = {len(in_specs): 0, len(in_specs) + 1: 1}
        operands += carried
        in_specs += [anywhere] * 2
    return pl.pallas_call(
        body,
        in_specs=in_specs,
        out_specs=[anywhere] * 2 + [vmem] * (n_groups + 1),
        out_shape=[
            *[jax.ShapeDtypeStruct((16, BLOCK, width), BF16)] * 2,
            *[jax.ShapeDtypeStruct((count * BLOCK, depth), BF16) for count in counts],
            jax.ShapeDtypeStruct((n_blocks, 8, width), F32),
        ],
        scratch_shapes=[pltpu.VMEM((n_blocks, BLOCK, width), BF16), pltpu.SemaphoreType.DMA((2 * n_blocks,))],
        input_output_aliases=aliases,
        compiler_params=PLAIN,
        cost_estimate=pl.CostEstimate(
            flops=2 * n_blocks * BLOCK * width * depth, bytes_accessed=n_blocks * 2 ** 20, transcendentals=0
        ),
    )(place, *operands)


ARRIVALS = [
    [[(False, 0, 0, 0, 0), (False, 0, 1, 1, 0), (False, 0, 3, 2, 0)], [(True, 0, 0, 3, 0), (True, 1, 0, 3, BLOCK)]],
    [
        [(False, 1, 0, 0, 0), (False, 1, 1, 1, 0), (False, 1, 3, 1, BLOCK)],
        [(True, 0, 1, 2, 0), (True, 1, 1, 2, BLOCK), (True, 0, 3, 3, 0), (True, 1, 3, 3, BLOCK)],
    ],
    [[(False, 0, 2, 0, 0), (False, 1, 2, 1, 0)], [(True, 0, 2, 2, 0), (True, 1, 2, 3, 0)]],
]


def split_grads(place, own, other, squares):
    width = own[0].shape[1]

    def body(place_ref, *refs):
        own_refs, other_refs, square_refs = refs[:3], refs[3:6], refs[6:9]
        up_ref, down_ref, rest_ref, sum_ref, grads_ref, parts_ref = refs[9:]
        for side, side_refs in ((1, own_refs), (0, other_refs)):
            for groups, ref, square_ref in zip(ARRIVALS, side_refs, square_refs):
                for i, (_, dz, dx, _, _) in enumerate(groups[side]):
                    k = half_block(place_ref, dz, dx)
                    part = ref[i * BLOCK : (i + 1) * BLOCK].astype(F32)
                    grads_ref[k] = part if side else grads_ref[k] + part
                    parts_ref[8 * side + k] = square_ref[i + side * len(groups[0])]
        total = parts_ref[0]
        for k in range(1, 16):
            total = total + parts_ref[k]
        sum_ref[...] = jnp.broadcast_to(jnp.sum(total), sum_ref.shape)

        def block(y_apart, z_apart):
            k = ((place_ref[0] + y_apart) & 3) * 2 + (place_ref[1] ^ z_apart)
            return grads_ref[k].astype(BF16)

        up_ref[:BLOCK] = block(2, 0)
        up_ref[BLOCK:] = block(1, 1)
        down_ref[:BLOCK] = block(2, 1)
        down_ref[BLOCK:] = block(3, 0)
        for i, (dy, dz) in enumerate(((1, 0), (3, 1), (0, 0), (0, 1))):
            rest_ref[i * BLOCK : (i + 1) * BLOCK] = block(dy, dz)

    return whole(
        body,
        [
            *[jax.ShapeDtypeStruct((n * BLOCK, width), BF16) for n in (2, 2, 4)],
            jax.ShapeDtypeStruct((8, BLOCK), F32),
        ],
        *own,
        *other,
        *squares,
        scalars=place,
        scratch=[pltpu.VMEM((8, BLOCK, width), F32), pltpu.VMEM((16, *squares[0].shape[1:]), F32)],
    )


def over_chips(values):
    groups = [[2 * i + core for i in range(8)] for core in range(2)]
    return lax.all_to_all(values, "dp", 0, 0, axis_index_groups=groups)


def on_device(
    teacher_hidden, attn_gain, w_query, key_projection, value_projection, w_out, student_hidden, w_proj
):
    tokens, width = teacher_hidden.shape
    dp = lax.axis_index("dp")
    tensor = lax.axis_index("tensor")
    core = dp % 2
    place = jnp.stack([dp // 4, (dp // 2) % 2, core, tensor // 4, tensor % 4])

    def student_unit(ref, dx, dz, parity):
        return 2 * half_block(ref, dz, dx) + parity

    student_far = products(place, student_hidden, w_proj, ORDERS_FAR, BLOCK, student_unit)
    w_proj_t = transposed(w_proj)
    unit = 2 * BLOCK
    student_up, student_down = send(student_far[0], X_UP), send(student_far[1], X_DOWN)

    student_next, student_prev, student_own = products(
        place, student_hidden, w_proj, ORDERS_NEAR, BLOCK, student_unit
    )

    weights = (w_query[0], key_projection[0], value_projection[0])
    right_sent = project(place, False, False, teacher_hidden, attn_gain, weights)
    right_got = send(right_sent, CORE)
    left_sent = project(place, False, True, teacher_hidden, attn_gain, weights[:1])
    left_got = send(left_sent, CORE)
    right = project(place, True, False, teacher_hidden, attn_gain, weights, right_got)
    right = over_chips(right.reshape(8, BLOCK, RIGHT))
    left = project(place, True, True, teacher_hidden, attn_gain, weights[:1], left_got)
    left, w_proj_t, student_next, student_prev, student_own, student_up, student_down = lax.optimization_barrier(
        (left, w_proj_t, student_next, student_prev, student_own, student_up, student_down)
    )
    student_next, student_prev = add_far(student_next, student_prev, student_up, student_down)
    student_up, student_down = send(student_next, X_UP), send(student_prev, X_DOWN)
    scale, queries_right, both = sum_right(right, left.reshape(8, BLOCK, LEFT))
    both = over_chips(both)
    student_row = add(student_own, student_up, student_down).astype(BF16)
    both, student_row = lax.optimization_barrier((both, student_row))
    kv_other = send(both[:, :, LEFT:], CORE)
    student_swap = send(student_row, ZLO)
    blended = attend(place, both, scale, queries_right, kv_other)
    blended, student_swap = lax.optimization_barrier((blended, student_swap))
    student_pair = add_swapped(student_row, student_swap)
    student_prev, student_next = send(student_pair, X_UP), send(student_pair, X_DOWN)

    heads_own = over_chips(blended)
    heads_own, student_prev, student_next = lax.optimization_barrier((heads_own, student_prev, student_next))
    heads_other = send(heads_own, CORE)
    out_weight = w_out[0]

    def half_of_block(ref, dz, dx, row):
        return 2 * half_block(ref, dz, dx) + row

    moved, moved_rest = products(place, heads_own, out_weight, ORDERS_Z[:2], HALF_BLOCK, half_of_block)
    moved, moved_rest, student_prev, student_next = lax.optimization_barrier(
        (moved, moved_rest, student_prev, student_next)
    )
    moved, moved_rest = send(moved, ZLO), send(moved_rest, ZLO)
    student_low = send(student_prev[:unit], X_UP)
    student_high = send(student_next[unit:], X_DOWN)
    up, down = products(place, heads_other, out_weight, ORDERS_X[:2], BLOCK, half_block)
    other_rest = products(place, heads_other, out_weight, ORDERS_X[2:], BLOCK, half_block)[0]
    kept, kept_rest = products(place, heads_own, out_weight, ORDERS_Z[2:], HALF_BLOCK, half_of_block)
    other_prev, other_next = send(up, X_UP), send(down, X_DOWN)
    moved, kept, kept_rest, student_low, student_high = lax.optimization_barrier(
        (moved, kept, kept_rest, student_low, student_high)
    )
    up = add(kept[:BLOCK], moved[:BLOCK]).astype(BF16)
    down = add(kept[BLOCK:], moved[BLOCK:]).astype(BF16)
    own_prev, own_next = send(up, X_UP), send(down, X_DOWN)
    low, high = ring_middle(other_rest, other_prev, other_next)
    low, high = send(low, X_UP), send(high, X_DOWN)
    own_rest = add(kept_rest, moved_rest)
    own_low, own_high = ring_middle(own_rest, own_prev, own_next)
    own_low, own_high, low, high = lax.optimization_barrier((own_low, own_high, low, high))
    own_low, own_high = send(own_low, X_UP), send(own_high, X_DOWN)
    low, high = ring_end(other_rest, other_prev, other_next, low, high)
    high = send(high.astype(BF16), ZLO)
    high, own_low, own_high = lax.optimization_barrier((high, own_low, own_high))

    def hidden_block(parity):
        return lax.dynamic_slice_in_dim(teacher_hidden, (2 * tensor + parity) * BLOCK, BLOCK).astype(F32)

    other_block = (hidden_block(1 - core) + low + high.astype(F32)).astype(BF16)
    own_sum = jnp.concatenate(ring_end(own_rest, own_prev, own_next, own_low, own_high))
    own_block = (hidden_block(core) + own_sum).astype(BF16)

    own_z, other_z = send(own_block, ZLO), send(other_block, ZLO)
    other_prev, other_next = send(other_block, X_UP), send(other_block, X_DOWN)
    own_z, other_prev, other_next = lax.optimization_barrier((own_z, other_prev, other_next))
    other_low, other_high = send(other_prev[:HALF_BLOCK], X_UP), send(other_next[HALF_BLOCK:], X_DOWN)
    own_pair = stack_rows(own_block, own_z)
    own_prev, own_next = send(own_pair, X_UP), send(own_pair, X_DOWN)
    other_sides = send(stack_rows(other_next, other_prev), ZLO)
    student = (student_pair, student_next, student_low, student_high, student_prev)
    results = [
        error_blocks(place, ARRIVALS[0], (other_block, other_next, other_prev, own_pair), student, w_proj_t)
    ]
    results[0], own_prev, own_next, other_low, other_high, other_sides, other_z = lax.optimization_barrier(
        (results[0], own_prev, own_next, other_low, other_high, other_sides, other_z)
    )
    other_far = stack_rows(other_low, other_high)
    other_far_z = send(other_far, ZLO)
    own_low, own_high = send(own_prev[:BLOCK], X_UP), send(own_next[BLOCK:], X_DOWN)
    pieces = (other_z, other_sides, own_next, own_prev)
    results.append(error_blocks(place, ARRIVALS[1], pieces, student, w_proj_t, results[0][:2]))
    results[1], other_far_z, own_low, own_high = lax.optimization_barrier((results[1], other_far_z, own_low, own_high))
    pieces = (other_far, other_far_z, own_low, own_high)
    results.append(error_blocks(place, ARRIVALS[2], pieces, student, w_proj_t, results[1][:2]))
    teacher_out, errors = results[2][:2]
    others = [send(result[2], CORE) for result in results]
    up, down, rest, loss = split_grads(place, [result[3] for result in results], others, [r[4] for r in results])
    proj_grad = lax.dot_general(
        student_hidden, errors.reshape(tokens, width), (((0,), (0,)), ((), ())), preferred_element_type=F32
    )
    proj_grad = proj_grad / tokens
    from_prev, from_next = send(up, Y_UP), send(down, Y_DOWN)
    losses = [send(loss, route) for route in (Y_FAR, Y_UP, Y_DOWN)]
    from_prev, from_next, *losses = lax.optimization_barrier((from_prev, from_next, *losses))
    loss = (loss + losses[0]) + (losses[1] + losses[2])
    low, high = ring_middle(rest, from_prev, from_next)
    low, high, loss_core = send(low, Y_UP), send(high, Y_DOWN), send(loss, CORE)
    low, high, loss_core, proj_grad = lax.optimization_barrier((low, high, loss_core, proj_grad))
    loss = loss + loss_core
    low, high = ring_end(rest, from_prev, from_next, low, high)
    high, loss_z = lax.optimization_barrier((send(high.astype(BF16), ZHI), send(loss, ZHI)))
    student_grad = low + high.astype(F32)
    distill_loss = (loss + loss_z)[0, 0] / (2.0 * tokens * MODEL_WIDTH)
    return (teacher_out.reshape(tokens, width), distill_loss, proj_grad, student_grad)


def solution(mesh):
    return jax.shard_map(
        on_device,
        mesh=mesh,
        in_specs=(
            P(None, "dp"),
            P(None, "dp"),
            P(None, "dp", "tensor"),
            P(None, "dp", "tensor"),
            P(None, "dp", "tensor"),
            P(None, "tensor", "dp"),
            P(None, "tensor"),
            P("tensor", "dp"),
        ),
        out_specs=(P(None, "dp"), P(), P("tensor", "dp"), P("dp", "tensor")),
        check_vma=False,
    )
```

```python
import math

import jax
import jax.numpy as jnp
from jax import lax
from jax.experimental import pallas as pl
from jax.experimental.pallas import tpu as pltpu
from jax.sharding import PartitionSpec as P

MODEL_WIDTH = 16384
HEAD_SIZE = 128
BLOCK = 128
EPSILON = 1e-05
F32 = jnp.float32
BF16 = jnp.bfloat16

CORE = ("dp", [(i, i ^ 1) for i in range(16)])
ZHI = ("dp", [(i, i ^ 2) for i in range(16)])
Y_FAR = ("dp", [(i, i ^ 8) for i in range(16)])
Y_UP = ("dp", [(i, (i + 4) % 16) for i in range(16)])
Y_DOWN = ("dp", [(i, (i - 4) % 16) for i in range(16)])
ZLO = ("tensor", [(t, t ^ 4) for t in range(8)])
CHIPS = [(dy, dz) for dy in range(4) for dz in range(2)]
TO_CHIP = {
    (dy, dz): ("dp", [(i, (i + 4 * dy) % 16 ^ (2 * dz)) for i in range(16)]) for dy, dz in CHIPS
}
X_UP = ("tensor", [(t, (t & 4) | ((t + 1) & 3)) for t in range(8)])
X_FAR = ("tensor", [(t, (t & 4) | ((t + 2) & 3)) for t in range(8)])
X_DOWN = ("tensor", [(t, (t & 4) | ((t - 1) & 3)) for t in range(8)])


def send(values, route):
    return lax.ppermute(values, route[0], route[1])


def matmul(left, right):
    return jnp.dot(left, right, preferred_element_type=F32)


def add(first, *others):
    total = first.astype(F32)
    for other in others:
        total = total + other.astype(F32)
    return total

VMEM_LIMIT = 56 * 1024 * 1024
PLAIN = pltpu.CompilerParams(vmem_limit_bytes=VMEM_LIMIT)


def whole(body, shapes, *operands, flops=0, scalars=None, scratch=()):
    size = sum(a.size * a.dtype.itemsize for a in operands)
    size += sum(math.prod(s.shape) * s.dtype.itemsize for s in shapes)
    in_specs = [pl.BlockSpec(memory_space=pltpu.VMEM)] * len(operands)
    if scalars is not None:
        in_specs = [pl.BlockSpec(memory_space=pltpu.SMEM)] + in_specs
        operands = (scalars, *operands)
    return pl.pallas_call(
        body,
        in_specs=in_specs,
        out_specs=[pl.BlockSpec(memory_space=pltpu.VMEM)] * len(shapes),
        out_shape=list(shapes),
        scratch_shapes=list(scratch),
        compiler_params=PLAIN,
        cost_estimate=pl.CostEstimate(flops=flops, bytes_accessed=size, transcendentals=0),
    )(*operands)


def stack_rows(*pieces):
    def body(*refs):
        start = 0
        for ref in refs[:-1]:
            refs[-1][start : start + ref.shape[0]] = ref[...]
            start += ref.shape[0]

    shape = jax.ShapeDtypeStruct((sum(p.shape[0] for p in pieces), pieces[0].shape[1]), pieces[0].dtype)
    return whole(body, (shape,), *pieces)[0]


def half_block(place_ref, z_apart, x_apart):
    return (place_ref[3] ^ z_apart) * 4 + ((place_ref[4] + x_apart) & 3)


def products(place, left, right, orders, unit, unit_of):
    units = left.reshape(-1, unit, left.shape[-1])

    def body(place_ref, left_ref, right_ref, *out_refs):
        rows = [left_ref[unit_of(place_ref, *which)] for order in orders for which in order]
        product = matmul(jnp.concatenate(rows), right_ref[...]).astype(BF16)
        start = 0
        for out_ref in out_refs:
            out_ref[...] = product[start : start + out_ref.shape[0]]
            start += out_ref.shape[0]

    shapes = [jax.ShapeDtypeStruct((len(order) * unit, right.shape[1]), BF16) for order in orders]
    flops = 2 * sum(len(order) for order in orders) * unit * right.size
    return whole(body, shapes, units, right, flops=flops, scalars=place)


LEFT = 6 * HEAD_SIZE
KV = 2 * HEAD_SIZE
SUMS = 4 * HEAD_SIZE
RIGHT = 5 * HEAD_SIZE


def project(place, mine, on_left, hidden, gain, weights, received=None):
    blocks = hidden.reshape(8, 2, BLOCK, hidden.shape[1])
    depth = hidden.shape[1]
    rows = 4 * BLOCK
    columns = LEFT if on_left else RIGHT
    n_weights = len(weights)

    def body(place_ref, hidden_ref, gain_ref, *refs):
        out_ref = refs[-1]
        values = hidden_ref[...].reshape(rows, depth).astype(F32)
        scaled = (values * gain_ref[...]).astype(BF16)
        parts = [ref[...] for ref in refs[:n_weights]]
        if not on_left:
            parts = [parts[0], jnp.concatenate(parts[1:], axis=1)]
        product = jnp.concatenate([matmul(scaled, part) for part in parts], axis=1)
        width = product.shape[1]
        if received is not None:
            got_ref = refs[n_weights]
            product = product + got_ref[:, :width].astype(F32)
        out_ref[:, :width] = product.astype(BF16)
        if on_left:
            return
        squares = jnp.sum(values * values, axis=1, keepdims=True)
        if received is not None:
            squares = squares + jnp.sum(got_ref[:, SUMS:].astype(F32), axis=1, keepdims=True)
        high = squares.astype(BF16).astype(F32)
        middle = (squares - high).astype(BF16).astype(F32)
        low = squares - high - middle
        column = lax.broadcasted_iota(jnp.int32, (rows, HEAD_SIZE), 1)
        spread = jnp.where(column == 0, high, jnp.where(column == 1, middle, jnp.where(column == 2, low, 0.0)))
        out_ref[:, SUMS:] = spread.astype(BF16)

    def fixed(shape, column=0):
        return pl.BlockSpec(shape, lambda i, place_ref: (0, column))

    query_spec = fixed((depth, LEFT)) if on_left else fixed((depth, KV), LEFT // KV)
    in_specs = [
        pl.BlockSpec((4, 1, BLOCK, depth), lambda i, place_ref: (i, place_ref[2] if mine else 1 - place_ref[2], 0, 0)),
        fixed(gain.shape),
        query_spec,
        *(fixed(w.shape) for w in weights[1:]),
    ]
    out_spec = pl.BlockSpec((rows, columns), lambda i, place_ref: (i, 0))
    operands = [blocks, gain, *weights]
    if received is not None:
        in_specs.append(out_spec)
        operands.append(received)
    return pl.pallas_call(
        body,
        grid_spec=pltpu.PrefetchScalarGridSpec(
            num_scalar_prefetch=1, grid=(2,), in_specs=in_specs, out_specs=out_spec
        ),
        out_shape=jax.ShapeDtypeStruct((8 * BLOCK, columns), BF16),
        compiler_params=PLAIN,
        cost_estimate=pl.CostEstimate(
            flops=2 * 8 * BLOCK * depth * columns, bytes_accessed=6 * 1024 * 1024, transcendentals=0
        ),
    )(place, *operands)


def sum_right(right, left):
    def body(right_ref, left_ref, scale_ref, queries_ref, both_ref):
        total = right_ref[0].astype(F32)
        for i in range(1, 8):
            total = total + right_ref[i].astype(F32)
        squares = jnp.sum(total[:, SUMS:], axis=1, keepdims=True)
        scale = lax.rsqrt(squares / MODEL_WIDTH + EPSILON)
        scale_ref[...] = jnp.broadcast_to(scale, (BLOCK, HEAD_SIZE))
        queries_ref[...] = (total[:, :KV] * scale).astype(BF16)
        key_value = (total[:, KV:SUMS] * scale).astype(BF16)
        both_ref[:, :, :LEFT] = left_ref[...]
        for i in range(8):
            both_ref[i, :, LEFT:] = key_value

    shapes = [
        jax.ShapeDtypeStruct((BLOCK, HEAD_SIZE), F32),
        jax.ShapeDtypeStruct((BLOCK, KV), BF16),
        jax.ShapeDtypeStruct((8, BLOCK, LEFT + KV), BF16),
    ]
    return whole(body, shapes, right, left)


def attend(place, both, scale, queries_right, kv_other):
    heads = LEFT // HEAD_SIZE + queries_right.shape[1] // HEAD_SIZE
    half = 8 * BLOCK

    def body(place_ref, both_ref, scale_ref, right_ref, other_ref, out_ref):
        y, z_hi, core = place_ref[0], place_ref[1], place_ref[2]
        shape = (2 * BLOCK, half)
        row = (y * 4 + z_hi * 2 + core) * BLOCK + lax.broadcasted_iota(jnp.int32, shape, 0) % BLOCK
        column = lax.broadcasted_iota(jnp.int32, shape, 1)
        spot = column // BLOCK * (2 * BLOCK) + column % BLOCK
        left_sum = both_ref[0, :, :LEFT].astype(F32)
        for i in range(1, 8):
            left_sum = left_sum + both_ref[i, :, :LEFT].astype(F32)
        left_queries = (left_sum * scale_ref[:, :1]).astype(BF16)
        sides = []
        own = both_ref[:, :, LEFT:].reshape(half, KV)
        other = other_ref[...].reshape(half, KV)
        for kv, parity in ((own, core), (other, 1 - core)):
            sides.append((kv[:, :HEAD_SIZE], kv[:, HEAD_SIZE:], spot + parity * BLOCK > row))
        for head in range(0, heads, 2):
            start = head * HEAD_SIZE
            pair = left_queries[:, start : start + KV] if start < LEFT else right_ref[...]
            query = jnp.concatenate((pair[:, :HEAD_SIZE], pair[:, HEAD_SIZE:]))
            scores = []
            for keys, _, hidden in sides:
                score = lax.dot_general(query, keys, (((1,), (1,)), ((), ())), preferred_element_type=F32)
                scores.append(jnp.where(hidden, -jnp.inf, score / math.sqrt(HEAD_SIZE)))
            top = jnp.maximum(*(jnp.max(s, axis=1, keepdims=True) for s in scores))
            weights = [jnp.exp(s - top) for s in scores]
            total = sum(jnp.sum(w, axis=1, keepdims=True) for w in weights)
            blended = sum(matmul(w.astype(BF16), side[1]) for w, side in zip(weights, sides))
            blended = (blended / total).astype(BF16)
            for i in range(8):
                out_ref[i, :, start : start + HEAD_SIZE] = blended[:BLOCK]
                out_ref[i, :, start + HEAD_SIZE : start + KV] = blended[BLOCK:]

    shape = jax.ShapeDtypeStruct((8, BLOCK, heads * HEAD_SIZE), BF16)
    operands = (both, scale, queries_right, kv_other)
    return whole(body, (shape,), *operands, flops=2 ** 30, scalars=place)[0]


def transposed(weight):
    def body(weight_ref, out_ref):
        out_ref[...] = weight_ref[...].T

    return whole(body, (jax.ShapeDtypeStruct(weight.shape[::-1], BF16),), weight)[0]


def add_far(following, previous, low, high):
    half = low.shape[0]

    def body(next_ref, previous_ref, low_ref, high_ref, up_ref, down_ref):
        up_ref[:half] = (next_ref[:half].astype(F32) + low_ref[...].astype(F32)).astype(BF16)
        up_ref[half:] = next_ref[half:]
        down_ref[:half] = previous_ref[:half]
        down_ref[half:] = (previous_ref[half:].astype(F32) + high_ref[...].astype(F32)).astype(BF16)

    shape = jax.ShapeDtypeStruct(following.shape, BF16)
    return whole(body, (shape, shape), following, previous, low, high)


def ring_middle(rest, from_prev, from_next):
    half = from_prev.shape[0] // 2
    return add(rest[:half], from_prev[:half]).astype(BF16), add(rest[half : 2 * half], from_next[:half]).astype(BF16)


def ring_end(rest, from_prev, from_next, low, high):
    half = from_prev.shape[0] // 2
    return (
        add(rest[2 * half : 3 * half], from_next[half:], low),
        add(rest[3 * half :], from_prev[half:], high),
    )


HALF_BLOCK = BLOCK // 2
UP_DOWN = [(2, 0), (1, 1), (2, 1), (3, 0)]
REST = [(1, 0), (3, 1), (0, 0), (0, 1)]
ORDERS_Z = [[(dz, dx, row) for dx, row in part] for dz in (1, 0) for part in (UP_DOWN, REST)]
ORDERS_X = [[(dz, dx) for dx, dz in part] for part in (UP_DOWN[:2], UP_DOWN[2:], REST)]
ORDERS_STUDENT = [
    [(dx, dz, parity) for dz in parts for parity in range(2)]
    for dx, parts in ((2, (0,)), (2, (1,)), (1, (0, 1)), (3, (0, 1)), (0, (0, 1)))
]
ORDERS_FAR, ORDERS_NEAR = ORDERS_STUDENT[:2], ORDERS_STUDENT[2:]


def error_blocks(place, groups, teacher, student, w_proj_t, carried=None):
    width, depth = w_proj_t.shape
    counts = [len(group) for group in groups]
    n_blocks, n_groups = sum(counts), len(groups)
    used = sorted({(dx, dz if dx == 2 else 0) for group in groups for _, dz, dx, _, _ in group})
    student = [student[(0, 1, 2 + dz, 4)[dx]] for dx, dz in used]
    n_teacher, n_student = len(teacher), len(student)

    def body(place_ref, *refs):
        teacher_refs, student_refs = refs[:n_teacher], refs[n_teacher : n_teacher + n_student]
        weight_ref = refs[n_teacher + n_student]
        out_ref, error_ref, *product_refs = refs[-5 - n_groups : -3]
        squares_ref, scratch_ref, sems = refs[-3:]
        copies = []

        def start_copy(source, target):
            copy = pltpu.make_async_copy(source, target, sems.at[len(copies)])
            copy.start()
            copies.append(copy)

        i = 0
        for group, product_ref in zip(groups, product_refs):
            first = i
            for mine, dz, dx, piece, start in group:
                parity = place_ref[2] if mine else 1 - place_ref[2]
                block = 2 * half_block(place_ref, dz, dx) + parity
                source = teacher_refs[piece]
                start_copy(source.at[pl.ds(start, BLOCK)], out_ref.at[block])
                values = source[start : start + BLOCK].astype(F32)
                if dx == 2:
                    source, start = student_refs[used.index((2, dz))], 0
                else:
                    source, start = student_refs[used.index((dx, 0))], dz * 2 * BLOCK
                target = source[pl.ds(pl.multiple_of(start + parity * BLOCK, BLOCK), BLOCK)]
                error = target.astype(F32) - values
                scratch_ref[i] = error.astype(BF16)
                start_copy(scratch_ref.at[i], error_ref.at[block])
                squares_ref[i] = jnp.sum((error * error).reshape(BLOCK // 8, 8, width), axis=0)
                i += 1
            errors = scratch_ref[first:i].reshape((i - first) * BLOCK, width)
            product_ref[...] = matmul(errors, weight_ref[...]).astype(BF16)
        for copy in copies:
            copy.wait()

    vmem, anywhere = pl.BlockSpec(memory_space=pltpu.VMEM), pl.BlockSpec(memory_space=pl.ANY)
    operands = [*teacher, *student, w_proj_t]
    in_specs = [pl.BlockSpec(memory_space=pltpu.SMEM)] + [vmem] * len(operands)
    aliases = {}
    if carried is not None:
        aliases = {len(in_specs): 0, len(in_specs) + 1: 1}
        operands += carried
        in_specs += [anywhere] * 2
    return pl.pallas_call(
        body,
        in_specs=in_specs,
        out_specs=[anywhere] * 2 + [vmem] * (n_groups + 1),
        out_shape=[
            *[jax.ShapeDtypeStruct((16, BLOCK, width), BF16)] * 2,
            *[jax.ShapeDtypeStruct((count * BLOCK, depth), BF16) for count in counts],
            jax.ShapeDtypeStruct((n_blocks, 8, width), F32),
        ],
        scratch_shapes=[pltpu.VMEM((n_blocks, BLOCK, width), BF16), pltpu.SemaphoreType.DMA((2 * n_blocks,))],
        input_output_aliases=aliases,
        compiler_params=PLAIN,
        cost_estimate=pl.CostEstimate(
            flops=2 * n_blocks * BLOCK * width * depth, bytes_accessed=n_blocks * 2 ** 20, transcendentals=0
        ),
    )(place, *operands)


ARRIVALS = [
    [[(False, 0, 0, 0, 0), (False, 0, 1, 1, 0), (False, 0, 3, 2, 0)], [(True, 0, 0, 3, 0), (True, 1, 0, 3, BLOCK)]],
    [
        [(False, 1, 0, 0, 0), (False, 1, 1, 1, 0), (False, 1, 3, 1, BLOCK)],
        [(True, 0, 1, 2, 0), (True, 1, 1, 2, BLOCK), (True, 0, 3, 3, 0), (True, 1, 3, 3, BLOCK)],
    ],
    [[(False, 0, 2, 0, 0), (False, 1, 2, 1, 0)], [(True, 0, 2, 2, 0), (True, 1, 2, 3, 0)]],
]


def split_grads(place, own, other, squares):
    width = own[0].shape[1]

    def body(place_ref, *refs):
        own_refs, other_refs, square_refs = refs[:3], refs[3:6], refs[6:9]
        up_ref, down_ref, rest_ref, sum_ref, grads_ref, parts_ref = refs[9:]
        for side, side_refs in ((1, own_refs), (0, other_refs)):
            for groups, ref, square_ref in zip(ARRIVALS, side_refs, square_refs):
                for i, (_, dz, dx, _, _) in enumerate(groups[side]):
                    k = half_block(place_ref, dz, dx)
                    part = ref[i * BLOCK : (i + 1) * BLOCK].astype(F32)
                    grads_ref[k] = part if side else grads_ref[k] + part
                    parts_ref[8 * side + k] = square_ref[i + side * len(groups[0])]
        total = parts_ref[0]
        for k in range(1, 16):
            total = total + parts_ref[k]
        sum_ref[...] = jnp.broadcast_to(jnp.sum(total), sum_ref.shape)

        def block(y_apart, z_apart):
            k = ((place_ref[0] + y_apart) & 3) * 2 + (place_ref[1] ^ z_apart)
            return grads_ref[k].astype(BF16)

        up_ref[:BLOCK] = block(2, 0)
        up_ref[BLOCK:] = block(1, 1)
        down_ref[:BLOCK] = block(2, 1)
        down_ref[BLOCK:] = block(3, 0)
        for i, (dy, dz) in enumerate(((1, 0), (3, 1), (0, 0), (0, 1))):
            rest_ref[i * BLOCK : (i + 1) * BLOCK] = block(dy, dz)

    return whole(
        body,
        [
            *[jax.ShapeDtypeStruct((n * BLOCK, width), BF16) for n in (2, 2, 4)],
            jax.ShapeDtypeStruct((8, BLOCK), F32),
        ],
        *own,
        *other,
        *squares,
        scalars=place,
        scratch=[pltpu.VMEM((8, BLOCK, width), F32), pltpu.VMEM((16, *squares[0].shape[1:]), F32)],
    )


def over_chips(values):
    groups = [[2 * i + core for i in range(8)] for core in range(2)]
    return lax.all_to_all(values, "dp", 0, 0, axis_index_groups=groups)


def on_device(
    teacher_hidden, attn_gain, w_query, key_projection, value_projection, w_out, student_hidden, w_proj
):
    tokens, width = teacher_hidden.shape
    dp = lax.axis_index("dp")
    tensor = lax.axis_index("tensor")
    core = dp % 2
    place = jnp.stack([dp // 4, (dp // 2) % 2, core, tensor // 4, tensor % 4])

    def student_unit(ref, dx, dz, parity):
        return 2 * half_block(ref, dz, dx) + parity

    student_far = products(place, student_hidden, w_proj, ORDERS_FAR, BLOCK, student_unit)
    w_proj_t = transposed(w_proj)
    unit = 2 * BLOCK
    student_up, student_down = send(student_far[0], X_UP), send(student_far[1], X_DOWN)

    student_next, student_prev, student_own = products(
        place, student_hidden, w_proj, ORDERS_NEAR, BLOCK, student_unit
    )

    weights = (w_query[0], key_projection[0], value_projection[0])
    right_sent = project(place, False, False, teacher_hidden, attn_gain, weights)
    right_got = send(right_sent, CORE)
    left_sent = project(place, False, True, teacher_hidden, attn_gain, weights[:1])
    left_got = send(left_sent, CORE)
    right = project(place, True, False, teacher_hidden, attn_gain, weights, right_got)
    right = over_chips(right.reshape(8, BLOCK, RIGHT))
    left = project(place, True, True, teacher_hidden, attn_gain, weights[:1], left_got)
    left, w_proj_t, student_next, student_prev, student_own, student_up, student_down = lax.optimization_barrier(
        (left, w_proj_t, student_next, student_prev, student_own, student_up, student_down)
    )
    student_next, student_prev = add_far(student_next, student_prev, student_up, student_down)
    right, student_next, student_prev = lax.optimization_barrier((right, student_next, student_prev))
    student_up, student_down = send(student_next, X_UP), send(student_prev, X_DOWN)
    scale, queries_right, both = sum_right(right, left.reshape(8, BLOCK, LEFT))
    both = over_chips(both)
    student_sum, student_other = (
        add(student_own[rows], student_up[rows], student_down[rows]) for rows in (slice(unit), slice(unit, None))
    )
    student_sum = add(student_sum, send(student_other.astype(BF16), ZLO)).astype(BF16)
    both, student_sum = lax.optimization_barrier((both, student_sum))
    kv_other = send(both[:, :, LEFT:], CORE)
    student_other = send(student_sum, ZLO)
    blended = attend(place, both, scale, queries_right, kv_other)
    blended, student_other = lax.optimization_barrier((blended, student_other))
    student_pair = stack_rows(student_sum, student_other)
    student_prev, student_next = send(student_pair, X_UP), send(student_pair, X_DOWN)

    heads_own = over_chips(blended)
    heads_own, student_prev, student_next = lax.optimization_barrier((heads_own, student_prev, student_next))
    heads_other = send(heads_own, CORE)
    out_weight = w_out[0]

    def half_of_block(ref, dz, dx, row):
        return 2 * half_block(ref, dz, dx) + row

    moved, moved_rest = products(place, heads_own, out_weight, ORDERS_Z[:2], HALF_BLOCK, half_of_block)
    moved, moved_rest, student_prev, student_next = lax.optimization_barrier(
        (moved, moved_rest, student_prev, student_next)
    )
    moved, moved_rest = send(moved, ZLO), send(moved_rest, ZLO)
    student_low = send(student_prev[:unit], X_UP)
    student_high = send(student_next[unit:], X_DOWN)
    up, down = products(place, heads_other, out_weight, ORDERS_X[:2], BLOCK, half_block)
    other_rest = products(place, heads_other, out_weight, ORDERS_X[2:], BLOCK, half_block)[0]
    kept, kept_rest = products(place, heads_own, out_weight, ORDERS_Z[2:], HALF_BLOCK, half_of_block)
    other_prev, other_next = send(up, X_UP), send(down, X_DOWN)
    moved, kept, kept_rest, student_low, student_high = lax.optimization_barrier(
        (moved, kept, kept_rest, student_low, student_high)
    )
    up = add(kept[:BLOCK], moved[:BLOCK]).astype(BF16)
    down = add(kept[BLOCK:], moved[BLOCK:]).astype(BF16)
    own_prev, own_next = send(up, X_UP), send(down, X_DOWN)
    low, high = ring_middle(other_rest, other_prev, other_next)
    low, high = send(low, X_UP), send(high, X_DOWN)
    own_rest = add(kept_rest, moved_rest)
    own_low, own_high = ring_middle(own_rest, own_prev, own_next)
    own_low, own_high, low, high = lax.optimization_barrier((own_low, own_high, low, high))
    own_low, own_high = send(own_low, X_UP), send(own_high, X_DOWN)
    low, high = ring_end(other_rest, other_prev, other_next, low, high)
    high = send(high.astype(BF16), ZLO)
    high, own_low, own_high = lax.optimization_barrier((high, own_low, own_high))

    def hidden_block(parity):
        return lax.dynamic_slice_in_dim(teacher_hidden, (2 * tensor + parity) * BLOCK, BLOCK).astype(F32)

    other_block = (hidden_block(1 - core) + low + high.astype(F32)).astype(BF16)
    own_sum = jnp.concatenate(ring_end(own_rest, own_prev, own_next, own_low, own_high))
    own_block = (hidden_block(core) + own_sum).astype(BF16)

    own_z, other_z = send(own_block, ZLO), send(other_block, ZLO)
    other_prev, other_next = send(other_block, X_UP), send(other_block, X_DOWN)
    own_z, other_prev, other_next = lax.optimization_barrier((own_z, other_prev, other_next))
    other_low, other_high = send(other_prev[:HALF_BLOCK], X_UP), send(other_next[HALF_BLOCK:], X_DOWN)
    own_pair = stack_rows(own_block, own_z)
    own_prev, own_next = send(own_pair, X_UP), send(own_pair, X_DOWN)
    other_sides = send(stack_rows(other_next, other_prev), ZLO)
    student = (student_pair, student_next, student_low, student_high, student_prev)
    results = [
        error_blocks(place, ARRIVALS[0], (other_block, other_next, other_prev, own_pair), student, w_proj_t)
    ]
    results[0], own_prev, own_next, other_low, other_high, other_sides, other_z = lax.optimization_barrier(
        (results[0], own_prev, own_next, other_low, other_high, other_sides, other_z)
    )
    other_far = stack_rows(other_low, other_high)
    other_far_z = send(other_far, ZLO)
    own_low, own_high = send(own_prev[:BLOCK], X_UP), send(own_next[BLOCK:], X_DOWN)
    pieces = (other_z, other_sides, own_next, own_prev)
    results.append(error_blocks(place, ARRIVALS[1], pieces, student, w_proj_t, results[0][:2]))
    results[1], other_far_z, own_low, own_high = lax.optimization_barrier((results[1], other_far_z, own_low, own_high))
    pieces = (other_far, other_far_z, own_low, own_high)
    results.append(error_blocks(place, ARRIVALS[2], pieces, student, w_proj_t, results[1][:2]))
    teacher_out, errors = results[2][:2]
    others = [send(result[2], CORE) for result in results]
    up, down, rest, loss = split_grads(place, [result[3] for result in results], others, [r[4] for r in results])
    proj_grad = lax.dot_general(
        student_hidden, errors.reshape(tokens, width), (((0,), (0,)), ((), ())), preferred_element_type=F32
    )
    proj_grad = proj_grad / tokens
    from_prev, from_next = send(up, Y_UP), send(down, Y_DOWN)
    losses = [send(loss, route) for route in (Y_FAR, Y_UP, Y_DOWN)]
    from_prev, from_next, *losses = lax.optimization_barrier((from_prev, from_next, *losses))
    loss = (loss + losses[0]) + (losses[1] + losses[2])
    low, high = ring_middle(rest, from_prev, from_next)
    low, high, loss_core = send(low, Y_UP), send(high, Y_DOWN), send(loss, CORE)
    low, high, loss_core, proj_grad = lax.optimization_barrier((low, high, loss_core, proj_grad))
    loss = loss + loss_core
    low, high = ring_end(rest, from_prev, from_next, low, high)
    high, loss_z = lax.optimization_barrier((send(high.astype(BF16), ZHI), send(loss, ZHI)))
    student_grad = low + high.astype(F32)
    distill_loss = (loss + loss_z)[0, 0] / (2.0 * tokens * MODEL_WIDTH)
    return (teacher_out.reshape(tokens, width), distill_loss, proj_grad, student_grad)


def solution(mesh):
    return jax.shard_map(
        on_device,
        mesh=mesh,
        in_specs=(
            P(None, "dp"),
            P(None, "dp"),
            P(None, "dp", "tensor"),
            P(None, "dp", "tensor"),
            P(None, "dp", "tensor"),
            P(None, "tensor", "dp"),
            P(None, "tensor"),
            P("tensor", "dp"),
        ),
        out_specs=(P(None, "dp"), P(), P("tensor", "dp"), P("dp", "tensor")),
        check_vma=False,
    )
```

```python
import math

import jax
import jax.numpy as jnp
from jax import lax
from jax.experimental import pallas as pl
from jax.experimental.pallas import tpu as pltpu
from jax.sharding import PartitionSpec as P

MODEL_WIDTH = 16384
HEAD_SIZE = 128
BLOCK = 128
EPSILON = 1e-05
F32 = jnp.float32
BF16 = jnp.bfloat16

CORE = ("dp", [(i, i ^ 1) for i in range(16)])
ZHI = ("dp", [(i, i ^ 2) for i in range(16)])
Y_FAR = ("dp", [(i, i ^ 8) for i in range(16)])
Y_UP = ("dp", [(i, (i + 4) % 16) for i in range(16)])
Y_DOWN = ("dp", [(i, (i - 4) % 16) for i in range(16)])
ZLO = ("tensor", [(t, t ^ 4) for t in range(8)])
CHIPS = [(dy, dz) for dy in range(4) for dz in range(2)]
TO_CHIP = {
    (dy, dz): ("dp", [(i, (i + 4 * dy) % 16 ^ (2 * dz)) for i in range(16)]) for dy, dz in CHIPS
}
X_UP = ("tensor", [(t, (t & 4) | ((t + 1) & 3)) for t in range(8)])
X_FAR = ("tensor", [(t, (t & 4) | ((t + 2) & 3)) for t in range(8)])
X_DOWN = ("tensor", [(t, (t & 4) | ((t - 1) & 3)) for t in range(8)])


def send(values, route):
    return lax.ppermute(values, route[0], route[1])


def matmul(left, right):
    return jnp.dot(left, right, preferred_element_type=F32)


def add(first, *others):
    total = first.astype(F32)
    for other in others:
        total = total + other.astype(F32)
    return total

VMEM_LIMIT = 56 * 1024 * 1024
PLAIN = pltpu.CompilerParams(vmem_limit_bytes=VMEM_LIMIT)


def whole(body, shapes, *operands, flops=0, scalars=None, scratch=()):
    size = sum(a.size * a.dtype.itemsize for a in operands)
    size += sum(math.prod(s.shape) * s.dtype.itemsize for s in shapes)
    in_specs = [pl.BlockSpec(memory_space=pltpu.VMEM)] * len(operands)
    if scalars is not None:
        in_specs = [pl.BlockSpec(memory_space=pltpu.SMEM)] + in_specs
        operands = (scalars, *operands)
    return pl.pallas_call(
        body,
        in_specs=in_specs,
        out_specs=[pl.BlockSpec(memory_space=pltpu.VMEM)] * len(shapes),
        out_shape=list(shapes),
        scratch_shapes=list(scratch),
        compiler_params=PLAIN,
        cost_estimate=pl.CostEstimate(flops=flops, bytes_accessed=size, transcendentals=0),
    )(*operands)


def stack_rows(*pieces):
    def body(*refs):
        start = 0
        for ref in refs[:-1]:
            refs[-1][start : start + ref.shape[0]] = ref[...]
            start += ref.shape[0]

    shape = jax.ShapeDtypeStruct((sum(p.shape[0] for p in pieces), pieces[0].shape[1]), pieces[0].dtype)
    return whole(body, (shape,), *pieces)[0]


def half_block(place_ref, z_apart, x_apart):
    return (place_ref[3] ^ z_apart) * 4 + ((place_ref[4] + x_apart) & 3)


def products(place, left, right, orders, unit, unit_of):
    units = left.reshape(-1, unit, left.shape[-1])

    def body(place_ref, left_ref, right_ref, *out_refs):
        rows = [left_ref[unit_of(place_ref, *which)] for order in orders for which in order]
        product = matmul(jnp.concatenate(rows), right_ref[...]).astype(BF16)
        start = 0
        for out_ref in out_refs:
            out_ref[...] = product[start : start + out_ref.shape[0]]
            start += out_ref.shape[0]

    shapes = [jax.ShapeDtypeStruct((len(order) * unit, right.shape[1]), BF16) for order in orders]
    flops = 2 * sum(len(order) for order in orders) * unit * right.size
    return whole(body, shapes, units, right, flops=flops, scalars=place)


LEFT = 6 * HEAD_SIZE
KV = 2 * HEAD_SIZE
SUMS = 4 * HEAD_SIZE
RIGHT = 5 * HEAD_SIZE


def project(place, mine, on_left, hidden, gain, weights, received=None):
    blocks = hidden.reshape(8, 2, BLOCK, hidden.shape[1])
    depth = hidden.shape[1]
    rows = 4 * BLOCK
    columns = LEFT if on_left else RIGHT
    n_weights = len(weights)

    def body(place_ref, hidden_ref, gain_ref, *refs):
        out_ref = refs[-1]
        values = hidden_ref[...].reshape(rows, depth).astype(F32)
        scaled = (values * gain_ref[...]).astype(BF16)
        parts = [ref[...] for ref in refs[:n_weights]]
        if not on_left:
            parts = [parts[0], jnp.concatenate(parts[1:], axis=1)]
        product = jnp.concatenate([matmul(scaled, part) for part in parts], axis=1)
        width = product.shape[1]
        if received is not None:
            got_ref = refs[n_weights]
            product = product + got_ref[:, :width].astype(F32)
        out_ref[:, :width] = product.astype(BF16)
        if on_left:
            return
        squares = jnp.sum(values * values, axis=1, keepdims=True)
        if received is not None:
            squares = squares + jnp.sum(got_ref[:, SUMS:].astype(F32), axis=1, keepdims=True)
        high = squares.astype(BF16).astype(F32)
        middle = (squares - high).astype(BF16).astype(F32)
        low = squares - high - middle
        column = lax.broadcasted_iota(jnp.int32, (rows, HEAD_SIZE), 1)
        spread = jnp.where(column == 0, high, jnp.where(column == 1, middle, jnp.where(column == 2, low, 0.0)))
        out_ref[:, SUMS:] = spread.astype(BF16)

    def fixed(shape, column=0):
        return pl.BlockSpec(shape, lambda i, place_ref: (0, column))

    query_spec = fixed((depth, LEFT)) if on_left else fixed((depth, KV), LEFT // KV)
    in_specs = [
        pl.BlockSpec((4, 1, BLOCK, depth), lambda i, place_ref: (i, place_ref[2] if mine else 1 - place_ref[2], 0, 0)),
        fixed(gain.shape),
        query_spec,
        *(fixed(w.shape) for w in weights[1:]),
    ]
    out_spec = pl.BlockSpec((rows, columns), lambda i, place_ref: (i, 0))
    operands = [blocks, gain, *weights]
    if received is not None:
        in_specs.append(out_spec)
        operands.append(received)
    return pl.pallas_call(
        body,
        grid_spec=pltpu.PrefetchScalarGridSpec(
            num_scalar_prefetch=1, grid=(2,), in_specs=in_specs, out_specs=out_spec
        ),
        out_shape=jax.ShapeDtypeStruct((8 * BLOCK, columns), BF16),
        compiler_params=PLAIN,
        cost_estimate=pl.CostEstimate(
            flops=2 * 8 * BLOCK * depth * columns, bytes_accessed=6 * 1024 * 1024, transcendentals=0
        ),
    )(place, *operands)


def sum_right(right, left):
    def body(right_ref, left_ref, scale_ref, queries_ref, both_ref):
        total = right_ref[0].astype(F32)
        for i in range(1, 8):
            total = total + right_ref[i].astype(F32)
        squares = jnp.sum(total[:, SUMS:], axis=1, keepdims=True)
        scale = lax.rsqrt(squares / MODEL_WIDTH + EPSILON)
        scale_ref[...] = jnp.broadcast_to(scale, (BLOCK, HEAD_SIZE))
        queries_ref[...] = (total[:, :KV] * scale).astype(BF16)
        key_value = (total[:, KV:SUMS] * scale).astype(BF16)
        both_ref[:, :, :LEFT] = left_ref[...]
        for i in range(8):
            both_ref[i, :, LEFT:] = key_value

    shapes = [
        jax.ShapeDtypeStruct((BLOCK, HEAD_SIZE), F32),
        jax.ShapeDtypeStruct((BLOCK, KV), BF16),
        jax.ShapeDtypeStruct((8, BLOCK, LEFT + KV), BF16),
    ]
    return whole(body, shapes, right, left)


def attend(place, both, scale, queries_right, kv_other):
    heads = LEFT // HEAD_SIZE + queries_right.shape[1] // HEAD_SIZE
    half = 8 * BLOCK

    def body(place_ref, both_ref, scale_ref, right_ref, other_ref, out_ref):
        y, z_hi, core = place_ref[0], place_ref[1], place_ref[2]
        shape = (2 * BLOCK, half)
        row = (y * 4 + z_hi * 2 + core) * BLOCK + lax.broadcasted_iota(jnp.int32, shape, 0) % BLOCK
        column = lax.broadcasted_iota(jnp.int32, shape, 1)
        spot = column // BLOCK * (2 * BLOCK) + column % BLOCK
        left_sum = both_ref[0, :, :LEFT].astype(F32)
        for i in range(1, 8):
            left_sum = left_sum + both_ref[i, :, :LEFT].astype(F32)
        left_queries = (left_sum * scale_ref[:, :1]).astype(BF16)
        sides = []
        own = both_ref[:, :, LEFT:].reshape(half, KV)
        other = other_ref[...].reshape(half, KV)
        for kv, parity in ((own, core), (other, 1 - core)):
            sides.append((kv[:, :HEAD_SIZE], kv[:, HEAD_SIZE:], spot + parity * BLOCK > row))
        for head in range(0, heads, 2):
            start = head * HEAD_SIZE
            pair = left_queries[:, start : start + KV] if start < LEFT else right_ref[...]
            query = jnp.concatenate((pair[:, :HEAD_SIZE], pair[:, HEAD_SIZE:]))
            scores = []
            for keys, _, hidden in sides:
                score = lax.dot_general(query, keys, (((1,), (1,)), ((), ())), preferred_element_type=F32)
                scores.append(jnp.where(hidden, -jnp.inf, score / math.sqrt(HEAD_SIZE)))
            top = jnp.maximum(*(jnp.max(s, axis=1, keepdims=True) for s in scores))
            weights = [jnp.exp(s - top) for s in scores]
            total = sum(jnp.sum(w, axis=1, keepdims=True) for w in weights)
            blended = sum(matmul(w.astype(BF16), side[1]) for w, side in zip(weights, sides))
            blended = (blended / total).astype(BF16)
            for i in range(8):
                out_ref[i, :, start : start + HEAD_SIZE] = blended[:BLOCK]
                out_ref[i, :, start + HEAD_SIZE : start + KV] = blended[BLOCK:]

    shape = jax.ShapeDtypeStruct((8, BLOCK, heads * HEAD_SIZE), BF16)
    operands = (both, scale, queries_right, kv_other)
    return whole(body, (shape,), *operands, flops=2 ** 30, scalars=place)[0]


def transposed(weight):
    def body(weight_ref, out_ref):
        out_ref[...] = weight_ref[...].T

    return whole(body, (jax.ShapeDtypeStruct(weight.shape[::-1], BF16),), weight)[0]


def add_far(following, previous, low, high):
    half = low.shape[0]

    def body(next_ref, previous_ref, low_ref, high_ref, up_ref, down_ref):
        up_ref[:half] = (next_ref[:half].astype(F32) + low_ref[...].astype(F32)).astype(BF16)
        up_ref[half:] = next_ref[half:]
        down_ref[:half] = previous_ref[:half]
        down_ref[half:] = (previous_ref[half:].astype(F32) + high_ref[...].astype(F32)).astype(BF16)

    shape = jax.ShapeDtypeStruct(following.shape, BF16)
    return whole(body, (shape, shape), following, previous, low, high)


def add_swapped(mine, theirs):
    half = mine.shape[0] // 2

    def body(mine_ref, theirs_ref, out_ref):
        out_ref[:half] = (mine_ref[:half].astype(F32) + theirs_ref[half:].astype(F32)).astype(BF16)
        out_ref[half:] = (mine_ref[half:].astype(F32) + theirs_ref[:half].astype(F32)).astype(BF16)

    return whole(body, (jax.ShapeDtypeStruct(mine.shape, BF16),), mine, theirs)[0]


def ring_middle(rest, from_prev, from_next):
    half = from_prev.shape[0] // 2
    return add(rest[:half], from_prev[:half]).astype(BF16), add(rest[half : 2 * half], from_next[:half]).astype(BF16)


def ring_end(rest, from_prev, from_next, low, high):
    half = from_prev.shape[0] // 2
    return (
        add(rest[2 * half : 3 * half], from_next[half:], low),
        add(rest[3 * half :], from_prev[half:], high),
    )


HALF_BLOCK = BLOCK // 2
UP_DOWN = [(2, 0), (1, 1), (2, 1), (3, 0)]
REST = [(1, 0), (3, 1), (0, 0), (0, 1)]
ORDERS_Z = [[(dz, dx, row) for dx, row in part] for dz in (1, 0) for part in (UP_DOWN, REST)]
ORDERS_X = [[(dz, dx) for dx, dz in part] for part in (UP_DOWN[:2], UP_DOWN[2:], REST)]
ORDERS_STUDENT = [
    [(dx, dz, parity) for dz in parts for parity in range(2)]
    for dx, parts in ((2, (0,)), (2, (1,)), (1, (0, 1)), (3, (0, 1)), (0, (0, 1)))
]
ORDERS_FAR, ORDERS_NEAR = ORDERS_STUDENT[:2], ORDERS_STUDENT[2:]


def error_blocks(place, groups, teacher, student, w_proj_t, carried=None):
    width, depth = w_proj_t.shape
    counts = [len(group) for group in groups]
    n_blocks, n_groups = sum(counts), len(groups)
    used = sorted({(dx, dz if dx == 2 else 0) for group in groups for _, dz, dx, _, _ in group})
    student = [student[(0, 1, 2 + dz, 4)[dx]] for dx, dz in used]
    n_teacher, n_student = len(teacher), len(student)

    def body(place_ref, *refs):
        teacher_refs, student_refs = refs[:n_teacher], refs[n_teacher : n_teacher + n_student]
        weight_ref = refs[n_teacher + n_student]
        out_ref, error_ref, *product_refs = refs[-5 - n_groups : -3]
        squares_ref, scratch_ref, sems = refs[-3:]
        copies = []

        def start_copy(source, target):
            copy = pltpu.make_async_copy(source, target, sems.at[len(copies)])
            copy.start()
            copies.append(copy)

        i = 0
        for group, product_ref in zip(groups, product_refs):
            first = i
            for mine, dz, dx, piece, start in group:
                parity = place_ref[2] if mine else 1 - place_ref[2]
                block = 2 * half_block(place_ref, dz, dx) + parity
                source = teacher_refs[piece]
                start_copy(source.at[pl.ds(start, BLOCK)], out_ref.at[block])
                values = source[start : start + BLOCK].astype(F32)
                if dx == 2:
                    source, start = student_refs[used.index((2, dz))], 0
                else:
                    source, start = student_refs[used.index((dx, 0))], dz * 2 * BLOCK
                target = source[pl.ds(pl.multiple_of(start + parity * BLOCK, BLOCK), BLOCK)]
                error = target.astype(F32) - values
                scratch_ref[i] = error.astype(BF16)
                start_copy(scratch_ref.at[i], error_ref.at[block])
                squares_ref[i] = jnp.sum((error * error).reshape(BLOCK // 8, 8, width), axis=0)
                i += 1
            errors = scratch_ref[first:i].reshape((i - first) * BLOCK, width)
            product_ref[...] = matmul(errors, weight_ref[...]).astype(BF16)
        for copy in copies:
            copy.wait()

    vmem, anywhere = pl.BlockSpec(memory_space=pltpu.VMEM), pl.BlockSpec(memory_space=pl.ANY)
    operands = [*teacher, *student, w_proj_t]
    in_specs = [pl.BlockSpec(memory_space=pltpu.SMEM)] + [vmem] * len(operands)
    aliases = {}
    if carried is not None:
        aliases = {len(in_specs): 0, len(in_specs) + 1: 1}
        operands += carried
        in_specs += [anywhere] * 2
    return pl.pallas_call(
        body,
        in_specs=in_specs,
        out_specs=[anywhere] * 2 + [vmem] * (n_groups + 1),
        out_shape=[
            *[jax.ShapeDtypeStruct((16, BLOCK, width), BF16)] * 2,
            *[jax.ShapeDtypeStruct((count * BLOCK, depth), BF16) for count in counts],
            jax.ShapeDtypeStruct((n_blocks, 8, width), F32),
        ],
        scratch_shapes=[pltpu.VMEM((n_blocks, BLOCK, width), BF16), pltpu.SemaphoreType.DMA((2 * n_blocks,))],
        input_output_aliases=aliases,
        compiler_params=PLAIN,
        cost_estimate=pl.CostEstimate(
            flops=2 * n_blocks * BLOCK * width * depth, bytes_accessed=n_blocks * 2 ** 20, transcendentals=0
        ),
    )(place, *operands)


ARRIVALS = [
    [[(False, 0, 0, 0, 0), (False, 0, 1, 1, 0), (False, 0, 3, 2, 0)], [(True, 0, 0, 3, 0), (True, 1, 0, 4, 0)]],
    [
        [(False, 1, 0, 0, 0), (False, 1, 1, 1, 0), (False, 1, 3, 1, BLOCK)],
        [(True, 0, 1, 2, 0), (True, 1, 1, 3, 0), (True, 0, 3, 4, 0), (True, 1, 3, 5, 0)],
    ],
    [[(False, 0, 2, 0, 0), (False, 1, 2, 1, 0)], [(True, 0, 2, 2, 0), (True, 1, 2, 3, 0)]],
]


def split_grads(place, own, other, squares):
    width = own[0].shape[1]

    def body(place_ref, *refs):
        own_refs, other_refs, square_refs = refs[:3], refs[3:6], refs[6:9]
        up_ref, down_ref, rest_ref, sum_ref, grads_ref, parts_ref = refs[9:]
        for side, side_refs in ((1, own_refs), (0, other_refs)):
            for groups, ref, square_ref in zip(ARRIVALS, side_refs, square_refs):
                for i, (_, dz, dx, _, _) in enumerate(groups[side]):
                    k = half_block(place_ref, dz, dx)
                    part = ref[i * BLOCK : (i + 1) * BLOCK].astype(F32)
                    grads_ref[k] = part if side else grads_ref[k] + part
                    parts_ref[8 * side + k] = square_ref[i + side * len(groups[0])]
        total = parts_ref[0]
        for k in range(1, 16):
            total = total + parts_ref[k]
        sum_ref[...] = jnp.broadcast_to(jnp.sum(total), sum_ref.shape)

        def block(y_apart, z_apart):
            k = ((place_ref[0] + y_apart) & 3) * 2 + (place_ref[1] ^ z_apart)
            return grads_ref[k].astype(BF16)

        up_ref[:BLOCK] = block(2, 0)
        up_ref[BLOCK:] = block(1, 1)
        down_ref[:BLOCK] = block(2, 1)
        down_ref[BLOCK:] = block(3, 0)
        for i, (dy, dz) in enumerate(((1, 0), (3, 1), (0, 0), (0, 1))):
            rest_ref[i * BLOCK : (i + 1) * BLOCK] = block(dy, dz)

    return whole(
        body,
        [
            *[jax.ShapeDtypeStruct((n * BLOCK, width), BF16) for n in (2, 2, 4)],
            jax.ShapeDtypeStruct((8, BLOCK), F32),
        ],
        *own,
        *other,
        *squares,
        scalars=place,
        scratch=[pltpu.VMEM((8, BLOCK, width), F32), pltpu.VMEM((16, *squares[0].shape[1:]), F32)],
    )


def over_chips(values):
    groups = [[2 * i + core for i in range(8)] for core in range(2)]
    return lax.all_to_all(values, "dp", 0, 0, axis_index_groups=groups)


def on_device(
    teacher_hidden, attn_gain, w_query, key_projection, value_projection, w_out, student_hidden, w_proj
):
    tokens, width = teacher_hidden.shape
    dp = lax.axis_index("dp")
    tensor = lax.axis_index("tensor")
    core = dp % 2
    place = jnp.stack([dp // 4, (dp // 2) % 2, core, tensor // 4, tensor % 4])

    def student_unit(ref, dx, dz, parity):
        return 2 * half_block(ref, dz, dx) + parity

    student_far = products(place, student_hidden, w_proj, ORDERS_FAR, BLOCK, student_unit)
    w_proj_t = transposed(w_proj)
    unit = 2 * BLOCK
    student_up, student_down = send(student_far[0], X_UP), send(student_far[1], X_DOWN)

    student_next, student_prev, student_own = products(
        place, student_hidden, w_proj, ORDERS_NEAR, BLOCK, student_unit
    )

    weights = (w_query[0], key_projection[0], value_projection[0])
    right_sent = project(place, False, False, teacher_hidden, attn_gain, weights)
    right_got = send(right_sent, CORE)
    left_sent = project(place, False, True, teacher_hidden, attn_gain, weights[:1])
    left_got = send(left_sent, CORE)
    right = project(place, True, False, teacher_hidden, attn_gain, weights, right_got)
    right = over_chips(right.reshape(8, BLOCK, RIGHT))
    left = project(place, True, True, teacher_hidden, attn_gain, weights[:1], left_got)
    left, w_proj_t, student_next, student_prev, student_own, student_up, student_down = lax.optimization_barrier(
        (left, w_proj_t, student_next, student_prev, student_own, student_up, student_down)
    )
    student_next, student_prev = add_far(student_next, student_prev, student_up, student_down)
    student_up, student_down = send(student_next, X_UP), send(student_prev, X_DOWN)
    scale, queries_right, both = sum_right(right, left.reshape(8, BLOCK, LEFT))
    both = over_chips(both)
    student_row = add(student_own, student_up, student_down).astype(BF16)
    both, student_row = lax.optimization_barrier((both, student_row))
    kv_other = send(both[:, :, LEFT:], CORE)
    student_swap = send(student_row, ZLO)
    blended = attend(place, both, scale, queries_right, kv_other)
    blended, student_swap = lax.optimization_barrier((blended, student_swap))
    student_pair = add_swapped(student_row, student_swap)
    student_prev, student_next = send(student_pair, X_UP), send(student_pair, X_DOWN)

    heads_own = over_chips(blended)
    heads_own, student_prev, student_next = lax.optimization_barrier((heads_own, student_prev, student_next))
    heads_other = send(heads_own, CORE)
    out_weight = w_out[0]

    def half_of_block(ref, dz, dx, row):
        return 2 * half_block(ref, dz, dx) + row

    moved, moved_rest = products(place, heads_own, out_weight, ORDERS_Z[:2], HALF_BLOCK, half_of_block)
    moved, moved_rest, student_prev, student_next = lax.optimization_barrier(
        (moved, moved_rest, student_prev, student_next)
    )
    moved, moved_rest = send(moved, ZLO), send(moved_rest, ZLO)
    student_low = send(student_prev[:unit], X_UP)
    student_high = send(student_next[unit:], X_DOWN)
    up, down = products(place, heads_other, out_weight, ORDERS_X[:2], BLOCK, half_block)
    other_rest = products(place, heads_other, out_weight, ORDERS_X[2:], BLOCK, half_block)[0]
    kept, kept_rest = products(place, heads_own, out_weight, ORDERS_Z[2:], HALF_BLOCK, half_of_block)
    other_prev, other_next = send(up, X_UP), send(down, X_DOWN)
    moved, kept, kept_rest, student_low, student_high = lax.optimization_barrier(
        (moved, kept, kept_rest, student_low, student_high)
    )
    up = add(kept[:BLOCK], moved[:BLOCK]).astype(BF16)
    down = add(kept[BLOCK:], moved[BLOCK:]).astype(BF16)
    own_prev, own_next = send(up, X_UP), send(down, X_DOWN)
    low, high = ring_middle(other_rest, other_prev, other_next)
    low, high = send(low, X_UP), send(high, X_DOWN)
    own_rest = add(kept_rest, moved_rest)
    own_low, own_high = ring_middle(own_rest, own_prev, own_next)
    own_low, own_high, low, high = lax.optimization_barrier((own_low, own_high, low, high))
    own_low, own_high = send(own_low, X_UP), send(own_high, X_DOWN)
    low, high = ring_end(other_rest, other_prev, other_next, low, high)
    high = send(high.astype(BF16), ZLO)
    high, own_low, own_high = lax.optimization_barrier((high, own_low, own_high))

    def hidden_block(parity):
        return lax.dynamic_slice_in_dim(teacher_hidden, (2 * tensor + parity) * BLOCK, BLOCK).astype(F32)

    other_block = (hidden_block(1 - core) + low + high.astype(F32)).astype(BF16)
    own_sum = jnp.concatenate(ring_end(own_rest, own_prev, own_next, own_low, own_high))
    own_block = (hidden_block(core) + own_sum).astype(BF16)

    other_prev, other_next = send(other_block, X_UP), send(other_block, X_DOWN)
    own_z, other_z = send(own_block, ZLO), send(other_block, ZLO)
    own_prev, own_next = send(own_block, X_UP), send(own_block, X_DOWN)
    own_z, other_prev, other_next = lax.optimization_barrier((own_z, other_prev, other_next))
    other_low, other_high = send(other_prev[:HALF_BLOCK], X_UP), send(other_next[HALF_BLOCK:], X_DOWN)
    own_prev_z, own_next_z = send(own_z, X_UP), send(own_z, X_DOWN)
    other_sides = send(stack_rows(other_next, other_prev), ZLO)
    student = (student_pair, student_next, student_low, student_high, student_prev)
    results = [
        error_blocks(place, ARRIVALS[0], (other_block, other_next, other_prev, own_block, own_z), student, w_proj_t)
    ]
    results[0], own_prev, own_next, own_prev_z, own_next_z, other_low, other_high, other_sides, other_z = (
        lax.optimization_barrier(
            (results[0], own_prev, own_next, own_prev_z, own_next_z, other_low, other_high, other_sides, other_z)
        )
    )
    other_far = stack_rows(other_low, other_high)
    other_far_z = send(other_far, ZLO)
    own_low, own_high = send(own_prev, X_UP), send(own_next_z, X_DOWN)
    pieces = (other_z, other_sides, own_next, own_next_z, own_prev, own_prev_z)
    results.append(error_blocks(place, ARRIVALS[1], pieces, student, w_proj_t, results[0][:2]))
    results[1], other_far_z, own_low, own_high = lax.optimization_barrier((results[1], other_far_z, own_low, own_high))
    pieces = (other_far, other_far_z, own_low, own_high)
    results.append(error_blocks(place, ARRIVALS[2], pieces, student, w_proj_t, results[1][:2]))
    teacher_out, errors = results[2][:2]
    others = [send(result[2], CORE) for result in results]
    up, down, rest, loss = split_grads(place, [result[3] for result in results], others, [r[4] for r in results])
    proj_grad = lax.dot_general(
        student_hidden, errors.reshape(tokens, width), (((0,), (0,)), ((), ())), preferred_element_type=F32
    )
    proj_grad = proj_grad / tokens
    from_prev, from_next = send(up, Y_UP), send(down, Y_DOWN)
    losses = [send(loss, route) for route in (Y_FAR, Y_UP, Y_DOWN)]
    from_prev, from_next, *losses = lax.optimization_barrier((from_prev, from_next, *losses))
    loss = (loss + losses[0]) + (losses[1] + losses[2])
    low, high = ring_middle(rest, from_prev, from_next)
    low, high, loss_core = send(low, Y_UP), send(high, Y_DOWN), send(loss, CORE)
    low, high, loss_core, proj_grad = lax.optimization_barrier((low, high, loss_core, proj_grad))
    loss = loss + loss_core
    low, high = ring_end(rest, from_prev, from_next, low, high)
    high, loss_z = lax.optimization_barrier((send(high.astype(BF16), ZHI), send(loss, ZHI)))
    student_grad = low + high.astype(F32)
    distill_loss = (loss + loss_z)[0, 0] / (2.0 * tokens * MODEL_WIDTH)
    return (teacher_out.reshape(tokens, width), distill_loss, proj_grad, student_grad)


def solution(mesh):
    return jax.shard_map(
        on_device,
        mesh=mesh,
        in_specs=(
            P(None, "dp"),
            P(None, "dp"),
            P(None, "dp", "tensor"),
            P(None, "dp", "tensor"),
            P(None, "dp", "tensor"),
            P(None, "tensor", "dp"),
            P(None, "tensor"),
            P("tensor", "dp"),
        ),
        out_specs=(P(None, "dp"), P(), P("tensor", "dp"), P("dp", "tensor")),
        check_vma=False,
    )
```

```python
import math

import jax
import jax.numpy as jnp
from jax import lax
from jax.experimental import pallas as pl
from jax.experimental.pallas import tpu as pltpu
from jax.sharding import PartitionSpec as P

MODEL_WIDTH = 16384
HEAD_SIZE = 128
BLOCK = 128
EPSILON = 1e-05
F32 = jnp.float32
BF16 = jnp.bfloat16

CORE = ("dp", [(i, i ^ 1) for i in range(16)])
ZHI = ("dp", [(i, i ^ 2) for i in range(16)])
CORE_ZHI = ("dp", [(i, i ^ 3) for i in range(16)])
Y_FAR = ("dp", [(i, i ^ 8) for i in range(16)])
Y_UP = ("dp", [(i, (i + 4) % 16) for i in range(16)])
Y_DOWN = ("dp", [(i, (i - 4) % 16) for i in range(16)])
ZLO = ("tensor", [(t, t ^ 4) for t in range(8)])
CHIPS = [(dy, dz) for dy in range(4) for dz in range(2)]
TO_CHIP = {
    (dy, dz): ("dp", [(i, (i + 4 * dy) % 16 ^ (2 * dz)) for i in range(16)]) for dy, dz in CHIPS
}
X_UP = ("tensor", [(t, (t & 4) | ((t + 1) & 3)) for t in range(8)])
X_FAR = ("tensor", [(t, (t & 4) | ((t + 2) & 3)) for t in range(8)])
X_DOWN = ("tensor", [(t, (t & 4) | ((t - 1) & 3)) for t in range(8)])


def send(values, route):
    return lax.ppermute(values, route[0], route[1])


def matmul(left, right):
    return jnp.dot(left, right, preferred_element_type=F32)


def add(first, *others):
    total = first.astype(F32)
    for other in others:
        total = total + other.astype(F32)
    return total

VMEM_LIMIT = 56 * 1024 * 1024
PLAIN = pltpu.CompilerParams(vmem_limit_bytes=VMEM_LIMIT)


def whole(body, shapes, *operands, flops=0, scalars=None, scratch=()):
    size = sum(a.size * a.dtype.itemsize for a in operands)
    size += sum(math.prod(s.shape) * s.dtype.itemsize for s in shapes)
    in_specs = [pl.BlockSpec(memory_space=pltpu.VMEM)] * len(operands)
    if scalars is not None:
        in_specs = [pl.BlockSpec(memory_space=pltpu.SMEM)] + in_specs
        operands = (scalars, *operands)
    return pl.pallas_call(
        body,
        in_specs=in_specs,
        out_specs=[pl.BlockSpec(memory_space=pltpu.VMEM)] * len(shapes),
        out_shape=list(shapes),
        scratch_shapes=list(scratch),
        compiler_params=PLAIN,
        cost_estimate=pl.CostEstimate(flops=flops, bytes_accessed=size, transcendentals=0),
    )(*operands)


def stack_rows(*pieces):
    def body(*refs):
        start = 0
        for ref in refs[:-1]:
            refs[-1][start : start + ref.shape[0]] = ref[...]
            start += ref.shape[0]

    shape = jax.ShapeDtypeStruct((sum(p.shape[0] for p in pieces), pieces[0].shape[1]), pieces[0].dtype)
    return whole(body, (shape,), *pieces)[0]


def half_block(place_ref, z_apart, x_apart):
    return (place_ref[3] ^ z_apart) * 4 + ((place_ref[4] + x_apart) & 3)


def products(place, left, right, orders, unit, unit_of):
    units = left.reshape(-1, unit, left.shape[-1])

    def body(place_ref, left_ref, right_ref, *out_refs):
        rows = [left_ref[unit_of(place_ref, *which)] for order in orders for which in order]
        product = matmul(jnp.concatenate(rows), right_ref[...]).astype(BF16)
        start = 0
        for out_ref in out_refs:
            out_ref[...] = product[start : start + out_ref.shape[0]]
            start += out_ref.shape[0]

    shapes = [jax.ShapeDtypeStruct((len(order) * unit, right.shape[1]), BF16) for order in orders]
    flops = 2 * sum(len(order) for order in orders) * unit * right.size
    return whole(body, shapes, units, right, flops=flops, scalars=place)


LEFT = 6 * HEAD_SIZE
KV = 2 * HEAD_SIZE
SUMS = 4 * HEAD_SIZE
RIGHT = 5 * HEAD_SIZE


def project(place, mine, on_left, hidden, gain, weights, received=None):
    blocks = hidden.reshape(8, 2, BLOCK, hidden.shape[1])
    depth = hidden.shape[1]
    rows = 4 * BLOCK
    columns = LEFT if on_left else RIGHT
    n_weights = len(weights)

    def body(place_ref, hidden_ref, gain_ref, *refs):
        out_ref = refs[-1]
        values = hidden_ref[...].reshape(rows, depth).astype(F32)
        scaled = (values * gain_ref[...]).astype(BF16)
        parts = [ref[...] for ref in refs[:n_weights]]
        if not on_left:
            parts = [parts[0], jnp.concatenate(parts[1:], axis=1)]
        product = jnp.concatenate([matmul(scaled, part) for part in parts], axis=1)
        width = product.shape[1]
        if received is not None:
            got_ref = refs[n_weights]
            product = product + got_ref[:, :width].astype(F32)
        out_ref[:, :width] = product.astype(BF16)
        if on_left:
            return
        squares = jnp.sum(values * values, axis=1, keepdims=True)
        if received is not None:
            squares = squares + jnp.sum(got_ref[:, SUMS:].astype(F32), axis=1, keepdims=True)
        high = squares.astype(BF16).astype(F32)
        middle = (squares - high).astype(BF16).astype(F32)
        low = squares - high - middle
        column = lax.broadcasted_iota(jnp.int32, (rows, HEAD_SIZE), 1)
        spread = jnp.where(column == 0, high, jnp.where(column == 1, middle, jnp.where(column == 2, low, 0.0)))
        out_ref[:, SUMS:] = spread.astype(BF16)

    def fixed(shape, column=0):
        return pl.BlockSpec(shape, lambda i, place_ref: (0, column))

    query_spec = fixed((depth, LEFT)) if on_left else fixed((depth, KV), LEFT // KV)
    in_specs = [
        pl.BlockSpec((4, 1, BLOCK, depth), lambda i, place_ref: (i, place_ref[2] if mine else 1 - place_ref[2], 0, 0)),
        fixed(gain.shape),
        query_spec,
        *(fixed(w.shape) for w in weights[1:]),
    ]
    out_spec = pl.BlockSpec((rows, columns), lambda i, place_ref: (i, 0))
    operands = [blocks, gain, *weights]
    if received is not None:
        in_specs.append(out_spec)
        operands.append(received)
    return pl.pallas_call(
        body,
        grid_spec=pltpu.PrefetchScalarGridSpec(
            num_scalar_prefetch=1, grid=(2,), in_specs=in_specs, out_specs=out_spec
        ),
        out_shape=jax.ShapeDtypeStruct((8 * BLOCK, columns), BF16),
        compiler_params=PLAIN,
        cost_estimate=pl.CostEstimate(
            flops=2 * 8 * BLOCK * depth * columns, bytes_accessed=6 * 1024 * 1024, transcendentals=0
        ),
    )(place, *operands)


def sum_right(right, left):
    def body(right_ref, left_ref, scale_ref, queries_ref, both_ref):
        total = right_ref[0].astype(F32)
        for i in range(1, 8):
            total = total + right_ref[i].astype(F32)
        squares = jnp.sum(total[:, SUMS:], axis=1, keepdims=True)
        scale = lax.rsqrt(squares / MODEL_WIDTH + EPSILON)
        scale_ref[...] = jnp.broadcast_to(scale, (BLOCK, HEAD_SIZE))
        queries_ref[...] = (total[:, :KV] * scale).astype(BF16)
        key_value = (total[:, KV:SUMS] * scale).astype(BF16)
        both_ref[:, :, :LEFT] = left_ref[...]
        for i in range(8):
            both_ref[i, :, LEFT:] = key_value

    shapes = [
        jax.ShapeDtypeStruct((BLOCK, HEAD_SIZE), F32),
        jax.ShapeDtypeStruct((BLOCK, KV), BF16),
        jax.ShapeDtypeStruct((8, BLOCK, LEFT + KV), BF16),
    ]
    return whole(body, shapes, right, left)


def attend(place, both, scale, queries_right, kv_other):
    heads = LEFT // HEAD_SIZE + queries_right.shape[1] // HEAD_SIZE
    half = 8 * BLOCK

    def body(place_ref, both_ref, scale_ref, right_ref, other_ref, out_ref):
        y, z_hi, core = place_ref[0], place_ref[1], place_ref[2]
        shape = (2 * BLOCK, half)
        row = (y * 4 + z_hi * 2 + core) * BLOCK + lax.broadcasted_iota(jnp.int32, shape, 0) % BLOCK
        column = lax.broadcasted_iota(jnp.int32, shape, 1)
        spot = column // BLOCK * (2 * BLOCK) + column % BLOCK
        left_sum = both_ref[0, :, :LEFT].astype(F32)
        for i in range(1, 8):
            left_sum = left_sum + both_ref[i, :, :LEFT].astype(F32)
        left_queries = (left_sum * scale_ref[:, :1]).astype(BF16)
        sides = []
        own = both_ref[:, :, LEFT:].reshape(half, KV)
        other = other_ref[...].reshape(half, KV)
        for kv, parity in ((own, core), (other, 1 - core)):
            sides.append((kv[:, :HEAD_SIZE], kv[:, HEAD_SIZE:], spot + parity * BLOCK > row))
        for head in range(0, heads, 2):
            start = head * HEAD_SIZE
            pair = left_queries[:, start : start + KV] if start < LEFT else right_ref[...]
            query = jnp.concatenate((pair[:, :HEAD_SIZE], pair[:, HEAD_SIZE:]))
            scores = []
            for keys, _, hidden in sides:
                score = lax.dot_general(query, keys, (((1,), (1,)), ((), ())), preferred_element_type=F32)
                scores.append(jnp.where(hidden, -jnp.inf, score / math.sqrt(HEAD_SIZE)))
            top = jnp.maximum(*(jnp.max(s, axis=1, keepdims=True) for s in scores))
            weights = [jnp.exp(s - top) for s in scores]
            total = sum(jnp.sum(w, axis=1, keepdims=True) for w in weights)
            blended = sum(matmul(w.astype(BF16), side[1]) for w, side in zip(weights, sides))
            blended = (blended / total).astype(BF16)
            for i in range(8):
                out_ref[i, :, start : start + HEAD_SIZE] = blended[:BLOCK]
                out_ref[i, :, start + HEAD_SIZE : start + KV] = blended[BLOCK:]

    shape = jax.ShapeDtypeStruct((8, BLOCK, heads * HEAD_SIZE), BF16)
    operands = (both, scale, queries_right, kv_other)
    return whole(body, (shape,), *operands, flops=2 ** 30, scalars=place)[0]


def transposed(weight):
    def body(weight_ref, out_ref):
        out_ref[...] = weight_ref[...].T

    return whole(body, (jax.ShapeDtypeStruct(weight.shape[::-1], BF16),), weight)[0]


def add_far(following, previous, low, high):
    half = low.shape[0]

    def body(next_ref, previous_ref, low_ref, high_ref, up_ref, down_ref):
        up_ref[:half] = (next_ref[:half].astype(F32) + low_ref[...].astype(F32)).astype(BF16)
        up_ref[half:] = next_ref[half:]
        down_ref[:half] = previous_ref[:half]
        down_ref[half:] = (previous_ref[half:].astype(F32) + high_ref[...].astype(F32)).astype(BF16)

    shape = jax.ShapeDtypeStruct(following.shape, BF16)
    return whole(body, (shape, shape), following, previous, low, high)


def add_swapped(mine, theirs):
    half = mine.shape[0] // 2

    def body(mine_ref, theirs_ref, out_ref):
        out_ref[:half] = (mine_ref[:half].astype(F32) + theirs_ref[half:].astype(F32)).astype(BF16)
        out_ref[half:] = (mine_ref[half:].astype(F32) + theirs_ref[:half].astype(F32)).astype(BF16)

    return whole(body, (jax.ShapeDtypeStruct(mine.shape, BF16),), mine, theirs)[0]


def ring_middle(rest, from_prev, from_next):
    half = from_prev.shape[0] // 2
    return add(rest[:half], from_prev[:half]).astype(BF16), add(rest[half : 2 * half], from_next[:half]).astype(BF16)


def ring_end(rest, from_prev, from_next, low, high):
    half = from_prev.shape[0] // 2
    return (
        add(rest[2 * half : 3 * half], from_next[half:], low),
        add(rest[3 * half :], from_prev[half:], high),
    )


HALF_BLOCK = BLOCK // 2
UP_DOWN = [(2, 0), (1, 1), (2, 1), (3, 0)]
REST = [(1, 0), (3, 1), (0, 0), (0, 1)]
ORDERS_Z = [[(dz, dx, row) for dx, row in part] for dz in (1, 0) for part in (UP_DOWN, REST)]
ORDERS_X = [[(dz, dx) for dx, dz in part] for part in (UP_DOWN[:2], UP_DOWN[2:], REST)]
ORDERS_STUDENT = [
    [(dx, dz, parity) for dz in parts for parity in range(2)]
    for dx, parts in ((2, (0,)), (2, (1,)), (1, (0, 1)), (3, (0, 1)), (0, (0, 1)))
]
ORDERS_FAR, ORDERS_NEAR = ORDERS_STUDENT[:2], ORDERS_STUDENT[2:]


def error_blocks(place, groups, teacher, student, w_proj_t, carried=None):
    width, depth = w_proj_t.shape
    counts = [len(group) for group in groups]
    n_blocks, n_groups = sum(counts), len(groups)
    used = sorted({(dx, dz if dx == 2 else 0) for group in groups for _, dz, dx, _, _ in group})
    student = [student[(0, 1, 2 + dz, 4)[dx]] for dx, dz in used]
    n_teacher, n_student = len(teacher), len(student)

    def body(place_ref, *refs):
        teacher_refs, student_refs = refs[:n_teacher], refs[n_teacher : n_teacher + n_student]
        weight_ref = refs[n_teacher + n_student]
        out_ref, error_ref, *product_refs = refs[-5 - n_groups : -3]
        squares_ref, scratch_ref, sems = refs[-3:]
        copies = []

        def start_copy(source, target):
            copy = pltpu.make_async_copy(source, target, sems.at[len(copies)])
            copy.start()
            copies.append(copy)

        i = 0
        for group, product_ref in zip(groups, product_refs):
            first = i
            for mine, dz, dx, piece, start in group:
                parity = place_ref[2] if mine else 1 - place_ref[2]
                block = 2 * half_block(place_ref, dz, dx) + parity
                source = teacher_refs[piece]
                start_copy(source.at[pl.ds(start, BLOCK)], out_ref.at[block])
                values = source[start : start + BLOCK].astype(F32)
                if dx == 2:
                    source, start = student_refs[used.index((2, dz))], 0
                else:
                    source, start = student_refs[used.index((dx, 0))], dz * 2 * BLOCK
                target = source[pl.ds(pl.multiple_of(start + parity * BLOCK, BLOCK), BLOCK)]
                error = target.astype(F32) - values
                scratch_ref[i] = error.astype(BF16)
                start_copy(scratch_ref.at[i], error_ref.at[block])
                squares_ref[i] = jnp.sum((error * error).reshape(BLOCK // 8, 8, width), axis=0)
                i += 1
            errors = scratch_ref[first:i].reshape((i - first) * BLOCK, width)
            product_ref[...] = matmul(errors, weight_ref[...]).astype(BF16)
        for copy in copies:
            copy.wait()

    vmem, anywhere = pl.BlockSpec(memory_space=pltpu.VMEM), pl.BlockSpec(memory_space=pl.ANY)
    operands = [*teacher, *student, w_proj_t]
    in_specs = [pl.BlockSpec(memory_space=pltpu.SMEM)] + [vmem] * len(operands)
    aliases = {}
    if carried is not None:
        aliases = {len(in_specs): 0, len(in_specs) + 1: 1}
        operands += carried
        in_specs += [anywhere] * 2
    return pl.pallas_call(
        body,
        in_specs=in_specs,
        out_specs=[anywhere] * 2 + [vmem] * (n_groups + 1),
        out_shape=[
            *[jax.ShapeDtypeStruct((16, BLOCK, width), BF16)] * 2,
            *[jax.ShapeDtypeStruct((count * BLOCK, depth), BF16) for count in counts],
            jax.ShapeDtypeStruct((n_blocks, 8, width), F32),
        ],
        scratch_shapes=[pltpu.VMEM((n_blocks, BLOCK, width), BF16), pltpu.SemaphoreType.DMA((2 * n_blocks,))],
        input_output_aliases=aliases,
        compiler_params=PLAIN,
        cost_estimate=pl.CostEstimate(
            flops=2 * n_blocks * BLOCK * width * depth, bytes_accessed=n_blocks * 2 ** 20, transcendentals=0
        ),
    )(place, *operands)


ARRIVALS = [
    [[(False, 0, 0, 0, 0), (False, 0, 1, 1, 0), (False, 0, 3, 2, 0)], [(True, 0, 0, 3, 0), (True, 1, 0, 3, BLOCK)]],
    [
        [(False, 1, 0, 0, 0), (False, 1, 1, 1, 0), (False, 1, 3, 1, BLOCK)],
        [(True, 0, 1, 2, 0), (True, 1, 1, 2, BLOCK), (True, 0, 3, 3, 0), (True, 1, 3, 3, BLOCK)],
    ],
    [[(False, 0, 2, 0, 0), (False, 1, 2, 1, 0)], [(True, 0, 2, 2, 0), (True, 1, 2, 3, 0)]],
]


def split_grads(place, own, other, squares):
    width = own[0].shape[1]

    def body(place_ref, *refs):
        own_refs, other_refs, square_refs = refs[:3], refs[3:6], refs[6:9]
        up_ref, down_ref, rest_ref, sum_ref, grads_ref, parts_ref = refs[9:]
        for side, side_refs in ((1, own_refs), (0, other_refs)):
            for groups, ref, square_ref in zip(ARRIVALS, side_refs, square_refs):
                for i, (_, dz, dx, _, _) in enumerate(groups[side]):
                    k = half_block(place_ref, dz, dx)
                    part = ref[i * BLOCK : (i + 1) * BLOCK].astype(F32)
                    grads_ref[k] = part if side else grads_ref[k] + part
                    parts_ref[8 * side + k] = square_ref[i + side * len(groups[0])]
        total = parts_ref[0]
        for k in range(1, 16):
            total = total + parts_ref[k]
        sum_ref[...] = jnp.broadcast_to(jnp.sum(total), sum_ref.shape)

        def block(y_apart, z_apart):
            k = ((place_ref[0] + y_apart) & 3) * 2 + (place_ref[1] ^ z_apart)
            return grads_ref[k].astype(BF16)

        up_ref[:BLOCK] = block(2, 0)
        up_ref[BLOCK:] = block(1, 1)
        down_ref[:BLOCK] = block(2, 1)
        down_ref[BLOCK:] = block(3, 0)
        for i, (dy, dz) in enumerate(((1, 0), (3, 1), (0, 0), (0, 1))):
            rest_ref[i * BLOCK : (i + 1) * BLOCK] = block(dy, dz)

    return whole(
        body,
        [
            *[jax.ShapeDtypeStruct((n * BLOCK, width), BF16) for n in (2, 2, 4)],
            jax.ShapeDtypeStruct((8, BLOCK), F32),
        ],
        *own,
        *other,
        *squares,
        scalars=place,
        scratch=[pltpu.VMEM((8, BLOCK, width), F32), pltpu.VMEM((16, *squares[0].shape[1:]), F32)],
    )


def over_chips(values):
    groups = [[2 * i + core for i in range(8)] for core in range(2)]
    return lax.all_to_all(values, "dp", 0, 0, axis_index_groups=groups)


def on_device(
    teacher_hidden, attn_gain, w_query, key_projection, value_projection, w_out, student_hidden, w_proj
):
    tokens, width = teacher_hidden.shape
    dp = lax.axis_index("dp")
    tensor = lax.axis_index("tensor")
    core = dp % 2
    place = jnp.stack([dp // 4, (dp // 2) % 2, core, tensor // 4, tensor % 4])

    def student_unit(ref, dx, dz, parity):
        return 2 * half_block(ref, dz, dx) + parity

    student_far = products(place, student_hidden, w_proj, ORDERS_FAR, BLOCK, student_unit)
    w_proj_t = transposed(w_proj)
    unit = 2 * BLOCK
    student_up, student_down = send(student_far[0], X_UP), send(student_far[1], X_DOWN)

    student_next, student_prev, student_own = products(
        place, student_hidden, w_proj, ORDERS_NEAR, BLOCK, student_unit
    )

    weights = (w_query[0], key_projection[0], value_projection[0])
    right_sent = project(place, False, False, teacher_hidden, attn_gain, weights)
    right_got = send(right_sent, CORE)
    left_sent = project(place, False, True, teacher_hidden, attn_gain, weights[:1])
    left_got = send(left_sent, CORE)
    right = project(place, True, False, teacher_hidden, attn_gain, weights, right_got)
    right = over_chips(right.reshape(8, BLOCK, RIGHT))
    left = project(place, True, True, teacher_hidden, attn_gain, weights[:1], left_got)
    left, w_proj_t, student_next, student_prev, student_own, student_up, student_down = lax.optimization_barrier(
        (left, w_proj_t, student_next, student_prev, student_own, student_up, student_down)
    )
    student_next, student_prev = add_far(student_next, student_prev, student_up, student_down)
    student_up, student_down = send(student_next, X_UP), send(student_prev, X_DOWN)
    scale, queries_right, both = sum_right(right, left.reshape(8, BLOCK, LEFT))
    both = over_chips(both)
    student_row = add(student_own, student_up, student_down).astype(BF16)
    both, student_row = lax.optimization_barrier((both, student_row))
    kv_other = send(both[:, :, LEFT:], CORE)
    student_swap = send(student_row, ZLO)
    blended = attend(place, both, scale, queries_right, kv_other)
    blended, student_swap = lax.optimization_barrier((blended, student_swap))
    student_pair = add_swapped(student_row, student_swap)
    student_prev, student_next = send(student_pair, X_UP), send(student_pair, X_DOWN)

    heads_own = over_chips(blended)
    heads_own, student_prev, student_next = lax.optimization_barrier((heads_own, student_prev, student_next))
    heads_other = send(heads_own, CORE)
    out_weight = w_out[0]

    def half_of_block(ref, dz, dx, row):
        return 2 * half_block(ref, dz, dx) + row

    moved, moved_rest = products(place, heads_own, out_weight, ORDERS_Z[:2], HALF_BLOCK, half_of_block)
    moved, moved_rest, student_prev, student_next = lax.optimization_barrier(
        (moved, moved_rest, student_prev, student_next)
    )
    moved, moved_rest = send(moved, ZLO), send(moved_rest, ZLO)
    student_low = send(student_prev[:unit], X_UP)
    student_high = send(student_next[unit:], X_DOWN)
    up, down = products(place, heads_other, out_weight, ORDERS_X[:2], BLOCK, half_block)
    other_rest = products(place, heads_other, out_weight, ORDERS_X[2:], BLOCK, half_block)[0]
    kept, kept_rest = products(place, heads_own, out_weight, ORDERS_Z[2:], HALF_BLOCK, half_of_block)
    other_prev, other_next = send(up, X_UP), send(down, X_DOWN)
    moved, kept, kept_rest, student_low, student_high = lax.optimization_barrier(
        (moved, kept, kept_rest, student_low, student_high)
    )
    up = add(kept[:BLOCK], moved[:BLOCK]).astype(BF16)
    down = add(kept[BLOCK:], moved[BLOCK:]).astype(BF16)
    own_prev, own_next = send(up, X_UP), send(down, X_DOWN)
    low, high = ring_middle(other_rest, other_prev, other_next)
    low, high = send(low, X_UP), send(high, X_DOWN)
    own_rest = add(kept_rest, moved_rest)
    own_low, own_high = ring_middle(own_rest, own_prev, own_next)
    own_low, own_high, low, high = lax.optimization_barrier((own_low, own_high, low, high))
    own_low, own_high = send(own_low, X_UP), send(own_high, X_DOWN)
    low, high = ring_end(other_rest, other_prev, other_next, low, high)
    high = send(high.astype(BF16), ZLO)
    high, own_low, own_high = lax.optimization_barrier((high, own_low, own_high))

    def hidden_block(parity):
        return lax.dynamic_slice_in_dim(teacher_hidden, (2 * tensor + parity) * BLOCK, BLOCK).astype(F32)

    other_block = (hidden_block(1 - core) + low + high.astype(F32)).astype(BF16)
    own_sum = jnp.concatenate(ring_end(own_rest, own_prev, own_next, own_low, own_high))
    own_block = (hidden_block(core) + own_sum).astype(BF16)

    own_z, other_z = send(own_block, ZLO), send(other_block, ZLO)
    other_prev, other_next = send(other_block, X_UP), send(other_block, X_DOWN)
    own_z, other_prev, other_next = lax.optimization_barrier((own_z, other_prev, other_next))
    other_low, other_high = send(other_prev[:HALF_BLOCK], X_UP), send(other_next[HALF_BLOCK:], X_DOWN)
    own_pair = stack_rows(own_block, own_z)
    own_prev, own_next = send(own_pair, X_UP), send(own_pair, X_DOWN)
    other_sides = send(stack_rows(other_next, other_prev), ZLO)
    student = (student_pair, student_next, student_low, student_high, student_prev)
    results = [
        error_blocks(place, ARRIVALS[0], (other_block, other_next, other_prev, own_pair), student, w_proj_t)
    ]
    results[0], own_prev, own_next, other_low, other_high, other_sides, other_z = lax.optimization_barrier(
        (results[0], own_prev, own_next, other_low, other_high, other_sides, other_z)
    )
    other_far = stack_rows(other_low, other_high)
    other_far_z = send(other_far, ZLO)
    own_low, own_high = send(own_prev[:BLOCK], X_UP), send(own_next[BLOCK:], X_DOWN)
    pieces = (other_z, other_sides, own_next, own_prev)
    results.append(error_blocks(place, ARRIVALS[1], pieces, student, w_proj_t, results[0][:2]))
    results[1], other_far_z, own_low, own_high = lax.optimization_barrier((results[1], other_far_z, own_low, own_high))
    pieces = (other_far, other_far_z, own_low, own_high)
    results.append(error_blocks(place, ARRIVALS[2], pieces, student, w_proj_t, results[1][:2]))
    teacher_out, errors = results[2][:2]
    others = [send(result[2], CORE) for result in results]
    up, down, rest, loss = split_grads(place, [result[3] for result in results], others, [r[4] for r in results])
    proj_grad = lax.dot_general(
        student_hidden, errors.reshape(tokens, width), (((0,), (0,)), ((), ())), preferred_element_type=F32
    )
    proj_grad = proj_grad / tokens
    from_prev, from_next = send(up, Y_UP), send(down, Y_DOWN)
    losses = [send(loss, route) for route in (Y_FAR, Y_UP, Y_DOWN)]
    from_prev, from_next = lax.optimization_barrier((from_prev, from_next))
    low, high = ring_middle(rest, from_prev, from_next)
    low, high = send(low, Y_UP), send(high, Y_DOWN)
    low, high, proj_grad, *losses = lax.optimization_barrier((low, high, proj_grad, *losses))
    low, high = ring_end(rest, from_prev, from_next, low, high)
    high = send(high.astype(BF16), ZHI)
    loss = (loss + losses[0]) + (losses[1] + losses[2])
    losses = [send(loss, route) for route in (CORE, ZHI, CORE_ZHI)]
    high, *losses = lax.optimization_barrier((high, *losses))
    student_grad = low + high.astype(F32)
    loss = (loss + losses[0]) + (losses[1] + losses[2])
    distill_loss = loss[0, 0] / (2.0 * tokens * MODEL_WIDTH)
    return (teacher_out.reshape(tokens, width), distill_loss, proj_grad, student_grad)


def solution(mesh):
    return jax.shard_map(
        on_device,
        mesh=mesh,
        in_specs=(
            P(None, "dp"),
            P(None, "dp"),
            P(None, "dp", "tensor"),
            P(None, "dp", "tensor"),
            P(None, "dp", "tensor"),
            P(None, "tensor", "dp"),
            P(None, "tensor"),
            P("tensor", "dp"),
        ),
        out_specs=(P(None, "dp"), P(), P("tensor", "dp"), P("dp", "tensor")),
        check_vma=False,
    )
```
